256 devices in a mesh: row: 16 (over z, x_hi), col: 16 (over y, x_lo, core).
Axes of the slice: x: 4 (x_hi: 2, x_lo: 2; x = x_hi * 2 + x_lo), y: 4, z: 8, core: 2. Of those that a mesh axis runs over, the one named last changes fastest.
Arguments:
- tokens: bfloat16 [2048, 8192], P('row', 'col'), may hold values from -6 to 6
- gate_weight: bfloat16 [8192, 28672], P('col', 'row'), may hold values from -0.0625 to 0.0625
- up_weight: bfloat16 [8192, 28672], P('col', 'row'), may hold values from -0.0625 to 0.0625
- down_weight: bfloat16 [28672, 8192], P('row', 'col'), may hold values from -0.078125 to 0.078125
- cotangent: bfloat16 [2048, 8192], P('row', 'col'), may hold values from -6 to 6
Outputs:
- mixed: bfloat16 [2048, 8192], P('row', 'col')
- grad_tokens: bfloat16 [2048, 8192], P('row', 'col')
- grad_gate: bfloat16 [8192, 28672], P('col', 'row')
- grad_up: bfloat16 [8192, 28672], P('col', 'row')
- grad_down: bfloat16 [28672, 8192], P('row', 'col')
The draws below stay inside these ranges and needn't reach their ends.
All inputs are finite; a program needn't handle non-finite values.
Results may differ from the reference program's by a relative error of at most 0.0049.
Values may be sent and summed in bfloat16 or wider, within the bound.
A program may use at most 128 MiB of HBM per device.

```python
import jax
import jax.numpy as jnp

D = 8192
FF = 28672
TOK_DEV = 128
STEPS = 3
TOKENS = 2048
HBLOCK = 1792
N_ROW = 16


def block_scale(own_key, shape, shards, low, high):
    def one(dim, shards_of):
        draws = jax.random.uniform(jax.random.fold_in(jax.random.fold_in(own_key, 6), dim), (shards_of,), jnp.float32, low / len(shards), high / len(shards))
        return jnp.repeat(jnp.exp(draws), shape[dim] // shards_of).reshape((-1,) + (1,) * (len(shape) - dim - 1))

    factor_of = one(*shards[0])
    for cut in shards[1:]:
        factor_of = factor_of * one(*cut)
    return factor_of


def bell_draw(key, shape, scale, reach, split=(), kind=jnp.bfloat16):
    values = jax.random.normal(key, shape, jnp.float32) * scale
    if len(split) > 0:
        values = block_scale(key, shape, split, -0.22, 0.18) * values
    return jnp.clip(values, min=-reach, max=reach).astype(kind)


def setup_inputs(seed: int = 0) -> dict:
    splits = jax.random.split(jax.random.key(seed), 6)
    tokens = bell_draw(splits[0], (TOKENS, D), 1.0, 6.0, ((0, 16), (1, 16)))
    gate_weight = bell_draw(splits[1], (D, FF), D ** -0.5, 0.0625, ((0, 16), (1, 16)))
    up_weight = bell_draw(splits[2], (D, FF), D ** -0.5, 0.0625, ((0, 16), (1, 16)))
    down_weight = bell_draw(splits[3], (FF, D), (STEPS * HBLOCK) ** -0.5, 0.078125, ((0, 16), (1, 16)))
    cotangent = bell_draw(splits[4], (TOKENS, D), 1.0, 6.0, ((0, 16), (1, 16)))
    return dict(tokens=tokens, gate_weight=gate_weight, up_weight=up_weight, down_weight=down_weight, cotangent=cotangent)


def reference(tokens, gate_weight, up_weight, down_weight, cotangent):
    width = FF // N_ROW
    out_sum = jnp.zeros((N_ROW, TOK_DEV, D), jnp.float32)
    grad_sum = jnp.zeros((N_ROW, TOK_DEV, D), jnp.float32)
    gate_cols = []
    up_cols = []
    down_rows = []
    for block in range(N_ROW):
        w_gate = gate_weight[:, block * width:(block + 1) * width]
        w_up = up_weight[:, block * width:(block + 1) * width]
        w_down = down_weight[block * width:(block + 1) * width, :]
        acc_gate = jnp.zeros((D, width), jnp.float32)
        acc_up = jnp.zeros((D, width), jnp.float32)
        acc_down = jnp.zeros((width, D), jnp.float32)
        for step in range(STEPS):
            owner = (block - step) % N_ROW
            rows_x = tokens[owner * TOK_DEV:(owner + 1) * TOK_DEV]
            rows_dy = cotangent[owner * TOK_DEV:(owner + 1) * TOK_DEV]
            gate = jnp.dot(rows_x, w_gate, preferred_element_type=jnp.float32)
            up = jnp.dot(rows_x, w_up, preferred_element_type=jnp.float32)
            sig = jax.nn.sigmoid(gate)
            act = gate * sig
            hidden = (act * up).astype(jnp.bfloat16)
            out_sum = out_sum.at[owner].add(jnp.dot(hidden, w_down, preferred_element_type=jnp.float32))
            grad_hidden = jnp.dot(rows_dy, w_down.T, preferred_element_type=jnp.float32)
            grad_g = (grad_hidden * up * sig * (1.0 + gate * (1.0 - sig))).astype(jnp.bfloat16)
            grad_u = (grad_hidden * act).astype(jnp.bfloat16)
            back = jnp.dot(grad_g, w_gate.T, preferred_element_type=jnp.float32)
            back = back + jnp.dot(grad_u, w_up.T, preferred_element_type=jnp.float32)
            grad_sum = grad_sum.at[owner].add(back)
            acc_gate = acc_gate + jnp.dot(rows_x.T, grad_g, preferred_element_type=jnp.float32)
            acc_up = acc_up + jnp.dot(rows_x.T, grad_u, preferred_element_type=jnp.float32)
            acc_down = acc_down + jnp.dot(hidden.T, rows_dy, preferred_element_type=jnp.float32)
        gate_cols.append(acc_gate.astype(jnp.bfloat16))
        up_cols.append(acc_up.astype(jnp.bfloat16))
        down_rows.append(acc_down.astype(jnp.bfloat16))
    mixed = out_sum.reshape(TOKENS, D).astype(jnp.bfloat16)
    grad_tokens = grad_sum.reshape(TOKENS, D).astype(jnp.bfloat16)
    return (mixed, grad_tokens, jnp.concatenate(gate_cols, axis=1), jnp.concatenate(up_cols, axis=1), jnp.concatenate(down_rows, axis=0))
```

```python
import functools

import jax
import jax.numpy as jnp
from jax import lax
from jax.experimental import pallas as pl
from jax.experimental.pallas import tpu as pltpu
from jax.sharding import PartitionSpec as P

MESH = pl.DeviceIdType.MESH
STEPS = 3
F32 = jnp.float32
BF16 = jnp.bfloat16

CORE_SUM = 0
Y_FAR = 3
Y_NEAR = 5
X_SUM = 9
X_GIVE = 10
Y_GIVE = 11
Y_PASS = 15
CORE_GIVE = 17
BACK = 25
FETCH = 26
KINDS = 28

SHIFTS = (0, 2, 1)
PARTS = ((0, 512), (512, 384))
TILE = 256
ORDER = (
    ("first", 0, 0),
    ("second", 0, 0),
    ("third", 0, 0),
    ("chip_sum", 0, 0),
    ("chip_sum", 0, 1),
    ("first", 1, 0),
    ("second", 1, 0),
    ("middle", 0, 0),
    ("third", 1, 0),
    ("middle", 0, 1),
    ("chip_sum", 1, 0),
    ("first", 2, 0),
    ("chip_sum", 1, 1),
    ("second", 2, 0),
    ("middle", 1, 0),
    ("third", 2, 0),
    ("cross", 0, 1),
    ("chip_sum", 2, 0),
    ("chip_sum", 2, 1),
    ("cross", 1, 0),
    ("middle", 1, 1),
    ("middle", 2, 0),
    ("activate", 0, 1),
    ("middle", 2, 1),
    ("activate", 1, 0),
    ("cross", 1, 1),
    ("cross", 2, 0),
    ("give_second", 1, 0),
    ("cross", 2, 1),
    ("activate", 1, 1),
    ("activate", 2, 0),
    ("activate", 2, 1),
    ("give_second", 1, 1),
    ("give_second", 2, 0),
    ("give_second", 2, 1),
    ("cross", 0, 0),
    ("pass_up", 1, 0),
    ("pass_down", 1, 0),
    ("pass_up", 2, 0),
    ("pass_down", 2, 0),
    ("pass_up", 2, 1),
    ("pass_down", 2, 1),
    ("pass_up", 1, 1),
    ("pass_down", 1, 1),
    ("activate", 0, 0),
    ("finish", 2, 0),
    ("finish", 1, 0),
    ("finish", 2, 1),
    ("give_second", 0, 0),
    ("finish", 1, 1),
    ("outputs", 2, 0),
    ("give_second", 0, 1),
    ("outputs", 1, 0),
    ("pass_down", 0, 0),
    ("pass_up", 0, 1),
    ("pass_down", 0, 1),
    ("pass_up", 0, 0),
    ("finish", 0, 1),
    ("finish", 0, 0),
    ("outputs", 0, 0),
    ("weights", 0, 0),
)


def shift_of(block):
    return SHIFTS[block]


def nn(a, b):
    return lax.dot_general(a, b, (((1,), (0,)), ((), ())), preferred_element_type=F32)


def nt(a, b):
    return lax.dot_general(a, b, (((1,), (1,)), ((), ())), preferred_element_type=F32)


def tn(a, b):
    return lax.dot_general(a, b, (((0,), (0,)), ((), ())), preferred_element_type=F32)


def exchange_kernel(
    n_row,
    n_y,
    tok,
    wg_hbm,
    wu_hbm,
    wd_hbm,
    cot,
    mixed_out,
    tokens_out,
    gate_hbm,
    up_hbm,
    down_hbm,
    wg,
    wu,
    wd,
    rows,
    core_out,
    core_in,
    total,
    total16,
    far_in,
    near_in,
    x_out,
    x_in,
    acts,
    own_end,
    back_out,
    back_in,
    gate_tile,
    up_tile,
    down_tile,
    send_sem,
    recv_sem,
    local_sem,
    out_sem,
):
    r = lax.axis_index("row")
    c = lax.axis_index("col")
    core = lax.rem(c, 2)
    xl = lax.rem(c // 2, 2)
    y = c // 4
    half = total.shape[-1]
    toks = rows.shape[2]
    span = far_in.shape[-2]

    def col(yy, xx, cc):
        return (yy * 2 + xx) * 2 + cc

    y_up = lax.rem(y + 1, n_y)
    y_down = lax.rem(y + n_y - 1, n_y)
    y_opp = lax.rem(y + 2, n_y)
    to_core = (r, col(y, xl, 1 - core))
    to_x = (r, col(y, 1 - xl, core))
    to_up = (r, col(y_up, xl, core))
    to_down = (r, col(y_down, xl, core))

    def to_row(by):
        return (lax.rem(r + n_row + by, n_row), c)

    def piece(yy, which):
        return yy * 2 + (xl if which == 0 else 1 - xl)

    def copy(src, dst, b, p, kind, device):
        return pltpu.make_async_remote_copy(
            src_ref=src,
            dst_ref=dst,
            send_sem=send_sem.at[b, p, kind],
            recv_sem=recv_sem.at[b, p, kind],
            device_id=device,
            device_id_type=MESH,
        )

    def recv(dst, b, p, kind):
        copy(dst, dst, b, p, kind, to_core).wait_recv()

    def sent(src, b, p, kind):
        copy(src, src, b, p, kind, to_core).wait_send()

    loads = [
        pltpu.make_async_copy(src, dst, local_sem.at[i])
        for i, (src, dst) in enumerate(((wg_hbm, wg), (wu_hbm, wu), (wd_hbm, wd)))
    ]
    own = [
        pltpu.make_async_copy(src, rows.at[SHIFTS.index(0), i], local_sem.at[3 + i])
        for i, src in enumerate((tok, cot))
    ]
    for load in own + loads:
        load.start()

    barrier = pltpu.get_barrier_semaphore()
    partners = [to_core, to_x, to_up, to_down] + [to_row(by) for by in (1, 2, -1, -2)]
    for partner in partners:
        pl.semaphore_signal(barrier, inc=1, device_id=partner, device_id_type=MESH)
    pl.semaphore_wait(barrier, len(partners))

    for b in range(STEPS):
        if shift_of(b) != 0:
            for i, src in enumerate((tok, cot)):
                copy(src, rows.at[b, i], b, 0, FETCH + i, to_row(shift_of(b))).start()
    for load in own + loads:
        load.wait()

    def half_of(which):
        return pl.ds(pl.multiple_of(which * half, 128), half)

    mine, other = half_of(core), half_of(1 - core)

    def lanes(p):
        return pl.ds(*PARTS[p])

    def wide(p, which):
        off, size = PARTS[p]
        return pl.ds(pl.multiple_of(which * half + off, 128), size)

    def product(b, i, where):
        if i < 2:
            part = nn(rows[b, 0], (wg, wu)[i][:, where])
        else:
            part = nt(rows[b, 1], wd[where, :])
        return part.reshape(total.shape[2:])

    def give_core(b, arrays):
        for i in arrays:
            core_out[b, i] = product(b, i, other)
            copy(core_out.at[b, i], core_in.at[b, i], b, 0, CORE_SUM + i, to_core).start()

    def first(b, p):
        if shift_of(b) != 0:
            recv(rows.at[b, 0], b, 0, FETCH)
        give_core(b, (0, 1))

    def second(b, p):
        if shift_of(b) != 0:
            recv(rows.at[b, 1], b, 0, FETCH + 1)
        give_core(b, (2,))

    def third(b, p):
        for i in range(3):
            total[b, i] = product(b, i, mine)

    def chip_sum(b, p):
        for i in range(3):
            if p == 0:
                recv(core_in.at[b, i], b, 0, CORE_SUM + i)
            value = total[b, i, :, :, lanes(p)] + core_in[b, i, :, :, lanes(p)]
            total[b, i, :, :, lanes(p)] = value
            total16[b, i, :, :, lanes(p)] = value.astype(BF16)
        for way, (device, which) in enumerate(((to_up, 0), (to_down, 1))):
            copy(
                total16.at[b, :, piece(y_opp, which), :, lanes(p)],
                far_in.at[b, way, :, :, lanes(p)],
                b, p, Y_FAR + way, device,
            ).start()
        for way, (device, yy, which) in enumerate(((to_up, y_up, 1), (to_down, y_down, 0))):
            near(b, p, way, which, piece(yy, which), device)

    def near(b, p, way, which, at, device):
        copy(
            total16.at[b, :, at, :, lanes(p)],
            near_in.at[b, way, which, :, :, lanes(p)],
            b, p, Y_NEAR + way * 2 + which, device,
        ).start()

    def middle(b, p):
        for way, (device, yy, which) in enumerate(((to_up, y_up, 0), (to_down, y_down, 1))):
            recv(far_in.at[b, way, :, :, lanes(p)], b, p, Y_FAR + way)
            at = piece(yy, which)
            value = total[b, :, at, :, lanes(p)] + far_in[b, way, :, :, lanes(p)].astype(F32)
            total16[b, :, at, :, lanes(p)] = value.astype(BF16)
            near(b, p, way, which, at, device)

    def y_sum(b, p, which):
        for way in range(2):
            recv(near_in.at[b, way, which, :, :, lanes(p)], b, p, Y_NEAR + way * 2 + which)
        return total[b, :, piece(y, which), :, lanes(p)] + (
            near_in[b, 0, which, :, :, lanes(p)].astype(F32)
            + near_in[b, 1, which, :, :, lanes(p)].astype(F32)
        )

    def cross(b, p):
        x_out[b, :, :, lanes(p)] = y_sum(b, p, 1).astype(x_out.dtype)
        copy(
            x_out.at[b, :, :, lanes(p)], x_in.at[b, :, :, lanes(p)], b, p, X_SUM, to_x
        ).start()

    def spot(b, at, where):
        return acts.at[b, :, pl.ds(pl.multiple_of(at * span, span), span), where]

    def give(b, p, yy, which, kind, device):
        ref = spot(b, piece(yy, which), wide(p, core))
        copy(ref, ref, b, p, kind, device).start()

    def take(b, p, yy, which, kind, side):
        recv(spot(b, piece(yy, which), wide(p, side)), b, p, kind)

    def activate(b, p):
        value = y_sum(b, p, 0)
        recv(x_in.at[b, :, :, lanes(p)], b, p, X_SUM)
        value = value + x_in[b, :, :, lanes(p)].astype(F32)
        gate, up, grad_hidden = value[0], value[1], value[2]
        sig = jax.nn.sigmoid(gate)
        act = gate * sig
        at = pl.ds(pl.multiple_of(piece(y, 0) * span, span), span)
        where = wide(p, core)
        acts[b, 0, at, where] = (act * up).astype(BF16)
        acts[b, 1, at, where] = (grad_hidden * up * sig * (1.0 + gate * (1.0 - sig))).astype(BF16)
        acts[b, 2, at, where] = (grad_hidden * act).astype(BF16)
        give(b, p, y, 0, X_GIVE, to_x)
        give(b, p, y, 0, Y_GIVE, to_up)
        give(b, p, y, 0, Y_GIVE + 2, to_down)
        give(b, p, y, 0, CORE_GIVE, to_core)

    def give_second(b, p):
        take(b, p, y, 1, X_GIVE, core)
        give(b, p, y, 1, Y_GIVE + 1, to_up)
        give(b, p, y, 1, Y_GIVE + 3, to_down)
        give(b, p, y, 1, CORE_GIVE + 1, to_core)

    def pass_up(b, p):
        take(b, p, y_down, 0, Y_GIVE, core)
        give(b, p, y_down, 0, Y_PASS, to_up)
        give(b, p, y_down, 0, CORE_GIVE + 6, to_core)
        take(b, p, y_up, 0, Y_GIVE + 2, core)
        give(b, p, y_up, 0, CORE_GIVE + 2, to_core)

    def pass_down(b, p):
        take(b, p, y_up, 1, Y_GIVE + 3, core)
        give(b, p, y_up, 1, Y_PASS + 1, to_down)
        give(b, p, y_up, 1, CORE_GIVE + 3, to_core)
        take(b, p, y_down, 1, Y_GIVE + 1, core)
        give(b, p, y_down, 1, CORE_GIVE + 7, to_core)

    def finish(b, p):
        for which in range(2):
            take(b, p, y_opp, which, Y_PASS + which, core)
            give(b, p, y_opp, which, CORE_GIVE + 4 + which, to_core)

    def outputs(b, p):
        for p in range(len(PARTS)):
            for k, yy in enumerate((y, y_up, y_opp, y_down)):
                for which in range(2):
                    take(b, p, yy, which, CORE_GIVE + 2 * k + which, 1 - core)
        mixed = nn(acts[b, 0], wd[...])
        back = nt(acts[b, 1], wg[...]) + nt(acts[b, 2], wu[...])
        if shift_of(b) != 0:
            back_out[b, 0] = mixed.astype(BF16)
            back_out[b, 1] = back.astype(BF16)
            copy(back_out.at[b], back_in.at[b], b, 0, BACK, to_row(-shift_of(b))).start()
        else:
            own_end[0] = mixed
            own_end[1] = back

    tiles = acts.shape[-1] // TILE

    def tile_of(i):
        return pl.ds(pl.multiple_of(i * TILE, TILE), TILE)

    def tile_copies(i):
        at = tile_of(i)
        return (
            pltpu.make_async_copy(gate_tile.at[i], gate_hbm.at[:, at], out_sem.at[i, 0]),
            pltpu.make_async_copy(up_tile.at[i], up_hbm.at[:, at], out_sem.at[i, 1]),
            pltpu.make_async_copy(down_tile.at[i], down_hbm.at[at, :], out_sem.at[i, 2]),
        )

    def weights(b, p):
        def one(i, carry):
            at = tile_of(i)
            x = rows[:, 0].reshape(STEPS * toks, -1)
            dy = rows[:, 1].reshape(STEPS * toks, -1)
            gate_tile[i] = tn(x, acts[:, 1, :, at].reshape(STEPS * toks, TILE)).astype(BF16)
            up_tile[i] = tn(x, acts[:, 2, :, at].reshape(STEPS * toks, TILE)).astype(BF16)
            down_tile[i] = tn(acts[:, 0, :, at].reshape(STEPS * toks, TILE), dy).astype(BF16)
            for out in tile_copies(i):
                out.start()
            return carry

        lax.fori_loop(0, tiles, one, 0)

    tasks = dict(
        first=first,
        second=second,
        third=third,
        chip_sum=chip_sum,
        middle=middle,
        cross=cross,
        activate=activate,
        give_second=give_second,
        pass_up=pass_up,
        pass_down=pass_down,
        finish=finish,
        outputs=outputs,
        weights=weights,
    )
    for name, b, p in ORDER:
        tasks[name](b, p)

    for i, out in enumerate((mixed_out, tokens_out)):
        value = own_end[i]
        for b in range(STEPS):
            if shift_of(b) != 0:
                if i == 0:
                    recv(back_in.at[b], b, 0, BACK)
                value = value + back_in[b, i].astype(F32)
        out[...] = value.astype(BF16)

    for b in range(STEPS):
        for i in range(3):
            sent(core_out.at[b, i], b, 0, CORE_SUM + i)
        for p in range(len(PARTS)):
            for way in range(2):
                sent(far_in.at[b, way, :, :, lanes(p)], b, p, Y_FAR + way)
                for which in range(2):
                    sent(near_in.at[b, way, which, :, :, lanes(p)], b, p, Y_NEAR + way * 2 + which)
            sent(x_out.at[b, :, :, lanes(p)], b, p, X_SUM)
            for kind in range(X_GIVE, CORE_GIVE + 8):
                sent(spot(b, piece(y, 0), wide(p, core)), b, p, kind)
        if shift_of(b) != 0:
            sent(back_out.at[b], b, 0, BACK)
            for i in range(2):
                sent(rows.at[b, i], b, 0, FETCH + i)

    def drain(i, carry):
        for out in tile_copies(i):
            out.wait()
        return carry

    lax.fori_loop(0, tiles, drain, 0)


def exchange(n_row, n_col, tokens, gate_weight, up_weight, down_weight, cotangent):
    toks, feats = tokens.shape
    hidden = gate_weight.shape[1]
    half = hidden // 2
    n_y = n_col // 4
    pieces = n_col // 2
    span = toks // pieces
    any_space = pl.BlockSpec(memory_space=pl.ANY)
    vmem = pl.BlockSpec(memory_space=pltpu.VMEM)
    return pl.pallas_call(
        functools.partial(exchange_kernel, n_row, n_y),
        out_shape=(
            jax.ShapeDtypeStruct((toks, feats), BF16),
            jax.ShapeDtypeStruct((toks, feats), BF16),
            jax.ShapeDtypeStruct((feats, hidden), BF16),
            jax.ShapeDtypeStruct((feats, hidden), BF16),
            jax.ShapeDtypeStruct((hidden, feats), BF16),
        ),
        in_specs=[any_space] * 5,
        out_specs=(vmem, vmem, any_space, any_space, any_space),
        scratch_shapes=[
            pltpu.VMEM(gate_weight.shape, BF16),
            pltpu.VMEM(up_weight.shape, BF16),
            pltpu.VMEM(down_weight.shape, BF16),
            pltpu.VMEM((STEPS, 2, toks, feats), BF16),
            pltpu.VMEM((STEPS, 3, pieces, span, half), F32),
            pltpu.VMEM((STEPS, 3, pieces, span, half), F32),
            pltpu.VMEM((STEPS, 3, pieces, span, half), F32),
            pltpu.VMEM((STEPS, 3, pieces, span, half), BF16),
            pltpu.VMEM((STEPS, 2, 3, span, half), BF16),
            pltpu.VMEM((STEPS, 2, 2, 3, span, half), BF16),
            pltpu.VMEM((STEPS, 3, span, half), BF16),
            pltpu.VMEM((STEPS, 3, span, half), BF16),
            pltpu.VMEM((STEPS, 3, toks, hidden), BF16),
            pltpu.VMEM((2, toks, feats), F32),
            pltpu.VMEM((STEPS, 2, toks, feats), BF16),
            pltpu.VMEM((STEPS, 2, toks, feats), BF16),
            pltpu.VMEM((hidden // TILE, feats, TILE), BF16),
            pltpu.VMEM((hidden // TILE, feats, TILE), BF16),
            pltpu.VMEM((hidden // TILE, TILE, feats), BF16),
            pltpu.SemaphoreType.DMA((STEPS, len(PARTS), KINDS)),
            pltpu.SemaphoreType.DMA((STEPS, len(PARTS), KINDS)),
            pltpu.SemaphoreType.DMA((5,)),
            pltpu.SemaphoreType.DMA((hidden // TILE, 3)),
        ],
        compiler_params=pltpu.CompilerParams(
            collective_id=0, has_side_effects=True, vmem_limit_bytes=60 * 2**20
        ),
        name="exchange",
    )(tokens, gate_weight, up_weight, down_weight, cotangent)


def solution(mesh):
    n_row, n_col = mesh.shape["row"], mesh.shape["col"]
    placed = (P("row", "col"), P("col", "row"), P("col", "row"), P("row", "col"), P("row", "col"))

    def body(tokens, gate_weight, up_weight, down_weight, cotangent):
        return exchange(n_row, n_col, tokens, gate_weight, up_weight, down_weight, cotangent)

    return jax.shard_map(
        body,
        mesh=mesh,
        in_specs=placed,
        out_specs=(
            P("row", "col"),
            P("row", "col"),
            P("col", "row"),
            P("col", "row"),
            P("row", "col"),
        ),
        check_vma=False,
    )
```

```python
import functools

import jax
import jax.numpy as jnp
from jax import lax
from jax.experimental import pallas as pl
from jax.experimental.pallas import tpu as pltpu
from jax.sharding import PartitionSpec as P

MESH = pl.DeviceIdType.MESH
STEPS = 3
F32 = jnp.float32
BF16 = jnp.bfloat16

CORE_SUM = 0
Y_FAR = 3
Y_NEAR = 5
X_SUM = 9
X_GIVE = 10
Y_GIVE = 11
Y_PASS = 15
CORE_GIVE = 17
BACK = 25
FETCH = 27
X_SUM_ALL = 29
X_GIVE_ALL = 33
KINDS = 37

SHIFTS = (0, 2, 1)
PARTS = ((0, 512), (512, 384))
X_FIRST = len(PARTS) - 1
TILE = 896
ORDER = (
    ("second", 0, 0),
    ("first", 0, 0),
    ("third", 0, 0),
    ("flip", 0, 0),
    ("chip_sum", 0, 1),
    ("chip_sum", 0, 0),
    ("arrive", 1, 0),
    ("first", 1, 0),
    ("arrive", 1, 1),
    ("middle", 0, 0),
    ("second", 1, 0),
    ("third", 1, 0),
    ("cross", 0, 1),
    ("chip_sum", 1, 1),
    ("chip_sum", 1, 0),
    ("arrive", 2, 0),
    ("first", 2, 0),
    ("arrive", 2, 1),
    ("second", 2, 0),
    ("middle", 0, 1),
    ("middle", 1, 0),
    ("third", 2, 0),
    ("cross", 0, 0),
    ("chip_sum", 2, 0),
    ("chip_sum", 2, 1),
    ("cross", 1, 1),
    ("middle", 2, 0),
    ("turn", 0, 0),
    ("cross", 1, 0),
    ("middle", 1, 1),
    ("activate", 0, 1),
    ("cross", 2, 1),
    ("cross", 2, 0),
    ("activate", 1, 0),
    ("turn", 1, 0),
    ("middle", 2, 1),
    ("activate", 1, 1),
    ("activate", 2, 0),
    ("flip", 2, 0),
    ("activate", 2, 1),
    ("pass_on", 1, 1),
    ("give_second", 2, 0),
    ("pass_on", 2, 1),
    ("swap_own", 1, 1),
    ("give_second", 1, 0),
    ("flip", 1, 0),
    ("pass_up", 2, 0),
    ("swap_near", 1, 1),
    ("pass_down", 2, 0),
    ("pass_up", 1, 0),
    ("finish_on", 2, 1),
    ("finish_on", 1, 1),
    ("pass_down", 1, 0),
    ("activate", 0, 0),
    ("swap_near", 2, 1),
    ("pass_on", 0, 1),
    ("swap_own", 2, 1),
    ("swap_far", 2, 1),
    ("swap_own", 0, 1),
    ("finish", 2, 0),
    ("swap_far", 1, 1),
    ("finish", 1, 0),
    ("outputs", 2, 0),
    ("give_second", 0, 0),
    ("outputs", 1, 0),
    ("pass_down", 0, 0),
    ("swap_near", 0, 1),
    ("turn", 2, 0),
    ("pass_up", 0, 0),
    ("finish_on", 0, 1),
    ("swap_far", 0, 1),
    ("weights", 2, 0),
    ("finish", 0, 0),
    ("outputs", 0, 0),
    ("weights", 1, 0),
    ("weights", 0, 0),
)


OWN, ONE, TWO = (SHIFTS.index(shift) for shift in range(STEPS))


def nn(a, b):
    return lax.dot_general(a, b, (((1,), (0,)), ((), ())), preferred_element_type=F32)


def nt(a, b):
    return lax.dot_general(a, b, (((1,), (1,)), ((), ())), preferred_element_type=F32)


def tn(a, b):
    return lax.dot_general(a, b, (((0,), (0,)), ((), ())), preferred_element_type=F32)


def exchange_kernel(
    n_row,
    n_y,
    tok,
    wg_hbm,
    wu_hbm,
    wd_hbm,
    cot,
    ends,
    acts_hbm,
    turned_hbm,
    cot_hbm,
    wg,
    wu,
    wd,
    wg_flip,
    wu_flip,
    wd_flip,
    rows,
    core_out,
    core_in,
    total,
    total16,
    far_in,
    near_in,
    x_out,
    x_in,
    x_all,
    acts,
    own_end,
    back_out,
    back_in,
    turned_x,
    turned_h,
    send_sem,
    recv_sem,
    local_sem,
    out_sem,
):
    r = lax.axis_index("row")
    c = lax.axis_index("col")
    core = lax.rem(c, 2)
    xl = lax.rem(c // 2, 2)
    y = c // 4
    half = total.shape[-1]
    toks = rows.shape[2]
    span = far_in.shape[-2]

    def col(yy, xx, cc):
        return (yy * 2 + xx) * 2 + cc

    y_up = lax.rem(y + 1, n_y)
    y_down = lax.rem(y + n_y - 1, n_y)
    y_opp = lax.rem(y + 2, n_y)
    to_core = (r, col(y, xl, 1 - core))
    to_x = (r, col(y, 1 - xl, core))
    to_up = (r, col(y_up, xl, core))
    to_down = (r, col(y_down, xl, core))

    y_on = lax.rem(y + 1 + 2 * core, n_y)
    y_off = lax.rem(y + 3 + 2 * core, n_y)
    to_on = (r, col(y_on, xl, core))
    to_off = (r, col(y_off, xl, core))
    chunks = (y, y_up, y_opp, y_down)

    def to_row(by):
        return (lax.rem(r + n_row + by, n_row), c)

    def piece(yy, which):
        return yy * 2 + (xl if which == 0 else 1 - xl)

    def copy(src, dst, b, p, kind, device):
        return pltpu.make_async_remote_copy(
            src_ref=src,
            dst_ref=dst,
            send_sem=send_sem.at[b, p, kind],
            recv_sem=recv_sem.at[b, p, kind],
            device_id=device,
            device_id_type=MESH,
        )

    def recv(dst, b, p, kind):
        copy(dst, dst, b, p, kind, to_core).wait_recv()

    def sent(src, b, p, kind):
        copy(src, src, b, p, kind, to_core).wait_send()

    def half_of(which):
        return pl.ds(pl.multiple_of(which * half, 128), half)

    mine, other = half_of(core), half_of(1 - core)

    loads = {}

    def load(name, src, dst):
        loads[name] = pltpu.make_async_copy(src, dst, local_sem.at[len(loads)])
        loads[name].start()

    def loaded(*names):
        for name in names:
            if name in loads:
                loads.pop(name).wait()

    load("x", tok, rows.at[OWN, 0])
    load("gate_other", wg_hbm.at[:, other], wg.at[:, other])
    load("up_other", wu_hbm.at[:, other], wu.at[:, other])
    load("dy", cot, rows.at[OWN, 1])
    load("down_other", wd_hbm.at[other], wd.at[other])
    load("gate_mine", wg_hbm.at[:, mine], wg.at[:, mine])
    load("up_mine", wu_hbm.at[:, mine], wu.at[:, mine])
    load("down_mine", wd_hbm.at[mine], wd.at[mine])

    barrier = pltpu.get_barrier_semaphore()
    partners = [to_core, to_x, to_up, to_down] + [to_row(by) for by in (1, 2, -1, -2)]
    for partner in partners:
        pl.semaphore_signal(barrier, inc=1, device_id=partner, device_id_type=MESH)
    pl.semaphore_wait(barrier, len(partners))

    first_of_pair = lax.rem(r, 2) == 0
    for i, src in enumerate((tok, cot)):
        copy(src, rows.at[TWO, i], TWO, 0, FETCH + i, to_row(2)).start()

    @pl.when(first_of_pair)
    def _():
        for i, src in enumerate((tok, cot)):
            copy(src, rows.at[ONE, i], ONE, 0, FETCH + i, to_row(1)).start()

    def arrive(b, i):
        recv(rows.at[b, i], b, 0, FETCH + i)
        if b == TWO:

            @pl.when(jnp.logical_not(first_of_pair))
            def _():
                copy(rows.at[b, i], rows.at[ONE, i], ONE, 0, FETCH + i, to_row(-1)).start()

    def lanes(p):
        return pl.ds(*PARTS[p])

    def wide(p, which):
        off, size = PARTS[p]
        return pl.ds(pl.multiple_of(which * half + off, 128), size)

    flipped = set()

    def flip(which, p):
        if which == 0:
            loaded("down_other", "down_mine")
            wd_flip[...] = wd[...].T
        elif which == 1:
            loaded("gate_other", "gate_mine")
            wg_flip[...] = wg[...].T
        else:
            loaded("up_other", "up_mine")
            wu_flip[...] = wu[...].T
        flipped.add(which)

    def product(b, i, where):
        if i < 2:
            part = nn(rows[b, 0], (wg, wu)[i][:, where])
        elif 0 in flipped:
            part = nn(rows[b, 1], wd_flip[:, where])
        else:
            part = nt(rows[b, 1], wd[where, :])
        return part.reshape(total.shape[2:])

    def give_core(b, arrays):
        for i in arrays:
            core_out[b, i] = product(b, i, other)
            copy(core_out.at[b, i], core_in.at[b, i], b, 0, CORE_SUM + i, to_core).start()

    def first(b, p):
        loaded("x", "gate_other", "up_other")
        give_core(b, (0, 1))

    def second(b, p):
        loaded("dy", "down_other")
        give_core(b, (2,))

    def third(b, p):
        loaded("gate_mine", "up_mine", "down_mine")
        for i in range(3):
            total[b, i] = product(b, i, mine)

    summed = set()

    def chip_sum(b, p):
        for i in range(3):
            if b not in summed:
                recv(core_in.at[b, i], b, 0, CORE_SUM + i)
            value = total[b, i, :, :, lanes(p)] + core_in[b, i, :, :, lanes(p)]
            total[b, i, :, :, lanes(p)] = value
            total16[b, i, :, :, lanes(p)] = value.astype(BF16)
        summed.add(b)
        if p == X_FIRST:
            for k, yy in enumerate(chunks):
                copy(
                    total16.at[b, :, piece(yy, 1), :, lanes(p)],
                    x_all.at[b, :, yy],
                    b, p, X_SUM_ALL + k, to_x,
                ).start()
            return
        for way, (device, which) in enumerate(((to_up, 0), (to_down, 1))):
            copy(
                total16.at[b, :, piece(y_opp, which), :, lanes(p)],
                far_in.at[b, way, :, :, lanes(p)],
                b, p, Y_FAR + way, device,
            ).start()
        for way, (device, yy, which) in enumerate(((to_up, y_up, 1), (to_down, y_down, 0))):
            near(b, p, way, which, piece(yy, which), device)

    def near(b, p, way, which, at, device):
        copy(
            total16.at[b, :, at, :, lanes(p)],
            near_in.at[b, way, which, :, :, lanes(p)],
            b, p, Y_NEAR + way * 2 + which, device,
        ).start()

    def middle(b, p):
        if p == X_FIRST:
            recv(far_in.at[b, 0, :, :, lanes(p)], b, p, Y_FAR)
            at = piece(y_on, 0)
            value = total[b, :, at, :, lanes(p)] + far_in[b, 0, :, :, lanes(p)].astype(F32)
            total16[b, :, at, :, lanes(p)] = value.astype(BF16)
            near(b, p, 0, 0, at, to_on)
            return
        for way, (device, yy, which) in enumerate(((to_up, y_up, 0), (to_down, y_down, 1))):
            recv(far_in.at[b, way, :, :, lanes(p)], b, p, Y_FAR + way)
            at = piece(yy, which)
            value = total[b, :, at, :, lanes(p)] + far_in[b, way, :, :, lanes(p)].astype(F32)
            total16[b, :, at, :, lanes(p)] = value.astype(BF16)
            near(b, p, way, which, at, device)

    def y_sum(b, p, which):
        for way in range(2):
            recv(near_in.at[b, way, which, :, :, lanes(p)], b, p, Y_NEAR + way * 2 + which)
        return total[b, :, piece(y, which), :, lanes(p)] + (
            near_in[b, 0, which, :, :, lanes(p)].astype(F32)
            + near_in[b, 1, which, :, :, lanes(p)].astype(F32)
        )

    def cross(b, p):
        if p == X_FIRST:
            for k, yy in enumerate(chunks):
                recv(x_all.at[b, :, yy], b, p, X_SUM_ALL + k)
                at = piece(yy, 0)
                value = total[b, :, at, :, lanes(p)] + x_all[b, :, yy].astype(F32)
                total[b, :, at, :, lanes(p)] = value
                if k != 0:
                    total16[b, :, at, :, lanes(p)] = value.astype(BF16)
            copy(
                total16.at[b, :, piece(y_opp, 0), :, lanes(p)],
                far_in.at[b, 0, :, :, lanes(p)],
                b, p, Y_FAR, to_on,
            ).start()
            near(b, p, 1, 0, piece(y_off, 0), to_off)
            return
        x_out[b, :, :, lanes(p)] = y_sum(b, p, 1).astype(x_out.dtype)
        copy(
            x_out.at[b, :, :, lanes(p)], x_in.at[b, :, :, lanes(p)], b, p, X_SUM, to_x
        ).start()

    def spot(b, at, where):
        return acts.at[b, :, pl.ds(pl.multiple_of(at * span, span), span), where]

    def give(b, p, yy, which, kind, device):
        ref = spot(b, piece(yy, which), wide(p, core))
        copy(ref, ref, b, p, kind, device).start()

    def take(b, p, yy, which, kind, side):
        recv(spot(b, piece(yy, which), wide(p, side)), b, p, kind)

    def activate(b, p):
        value = y_sum(b, p, 0)
        if p != X_FIRST:
            recv(x_in.at[b, :, :, lanes(p)], b, p, X_SUM)
            value = value + x_in[b, :, :, lanes(p)].astype(F32)
        gate, up, grad_hidden = value[0], value[1], value[2]
        sig = jax.nn.sigmoid(gate)
        act = gate * sig
        at = pl.ds(pl.multiple_of(piece(y, 0) * span, span), span)
        where = wide(p, core)
        acts[b, 0, at, where] = (act * up).astype(BF16)
        acts[b, 1, at, where] = (grad_hidden * up * sig * (1.0 + gate * (1.0 - sig))).astype(BF16)
        acts[b, 2, at, where] = (grad_hidden * act).astype(BF16)
        give(b, p, y, 0, X_GIVE_ALL if p == X_FIRST else X_GIVE, to_x)
        give(b, p, y, 0, Y_GIVE, to_up)
        give(b, p, y, 0, Y_GIVE + 2, to_down)
        give(b, p, y, 0, CORE_GIVE, to_core)

    def give_second(b, p):
        take(b, p, y, 1, X_GIVE, core)
        give(b, p, y, 1, Y_GIVE + 1, to_up)
        give(b, p, y, 1, Y_GIVE + 3, to_down)
        give(b, p, y, 1, CORE_GIVE + 1, to_core)

    def swap(b, p, ks):
        for k in ks:
            take(b, p, chunks[k], 1, X_GIVE_ALL + k, core)
            give(b, p, chunks[k], 1, CORE_GIVE + 2 * k + 1, to_core)

    def swap_own(b, p):
        swap(b, p, (0,))

    def swap_near(b, p):
        swap(b, p, (1, 3))

    def swap_far(b, p):
        swap(b, p, (2,))

    def pass_on(b, p):
        take(b, p, y_down, 0, Y_GIVE, core)
        take(b, p, y_up, 0, Y_GIVE + 2, core)
        give(b, p, y_off, 0, Y_PASS, to_on)
        for k in (1, 3):
            give(b, p, chunks[k], 0, X_GIVE_ALL + k, to_x)
            give(b, p, chunks[k], 0, CORE_GIVE + 2 * k, to_core)

    def finish_on(b, p):
        take(b, p, y_opp, 0, Y_PASS, core)
        give(b, p, y_opp, 0, X_GIVE_ALL + 2, to_x)
        give(b, p, y_opp, 0, CORE_GIVE + 4, to_core)

    def pass_up(b, p):
        take(b, p, y_down, 0, Y_GIVE, core)
        give(b, p, y_down, 0, Y_PASS, to_up)
        give(b, p, y_down, 0, CORE_GIVE + 6, to_core)
        take(b, p, y_up, 0, Y_GIVE + 2, core)
        give(b, p, y_up, 0, CORE_GIVE + 2, to_core)

    def pass_down(b, p):
        take(b, p, y_up, 1, Y_GIVE + 3, core)
        give(b, p, y_up, 1, Y_PASS + 1, to_down)
        give(b, p, y_up, 1, CORE_GIVE + 3, to_core)
        take(b, p, y_down, 1, Y_GIVE + 1, core)
        give(b, p, y_down, 1, CORE_GIVE + 7, to_core)

    def finish(b, p):
        for which in range(2):
            take(b, p, y_opp, which, Y_PASS + which, core)
            give(b, p, y_opp, which, CORE_GIVE + 4 + which, to_core)

    def outputs(b, p):
        for p in range(len(PARTS)):
            for k, yy in enumerate((y, y_up, y_opp, y_down)):
                for which in range(2):
                    take(b, p, yy, which, CORE_GIVE + 2 * k + which, 1 - core)
        for i in range(2):
            if i == 0:
                value = nn(acts[b, 0], wd[...])
            else:
                value = nn(acts[b, 1], wg_flip[...]) + nn(acts[b, 2], wu_flip[...])
            if b == OWN:
                own_end[i] = value
            else:
                back_out[b, i] = value.astype(BF16)
                copy(
                    back_out.at[b, i], back_in.at[b, i], b, 0, BACK + i, to_row(-SHIFTS[b])
                ).start()

    def stores(b):
        at = pl.ds(b * toks, toks)
        hidden = turned_h.shape[1]
        return tuple(
            pltpu.make_async_copy(src, dst, out_sem.at[b, i])
            for i, (src, dst) in enumerate(
                (
                    (acts.at[b, pl.ds(1, 2)], acts_hbm.at[:, at]),
                    (turned_h.at[b], turned_hbm.at[b, pl.ds(0, hidden)]),
                    (turned_x.at[b], turned_hbm.at[b, pl.ds(hidden, turned_x.shape[1])]),
                    (rows.at[b, 1], cot_hbm.at[at]),
                )
            )
        )

    def turn(b, p):
        turned_x[b] = rows[b, 0].T

    def weights(b, p):
        at_once, after_turn, *rest = stores(b)
        at_once.start()
        for store in rest:
            store.start()
        turned_h[b] = acts[b, 0].T
        after_turn.start()

    tasks = dict(
        flip=flip,
        arrive=arrive,
        first=first,
        second=second,
        third=third,
        chip_sum=chip_sum,
        middle=middle,
        cross=cross,
        activate=activate,
        give_second=give_second,
        swap_own=swap_own,
        swap_near=swap_near,
        swap_far=swap_far,
        pass_on=pass_on,
        finish_on=finish_on,
        pass_up=pass_up,
        pass_down=pass_down,
        finish=finish,
        outputs=outputs,
        turn=turn,
        weights=weights,
    )
    for name, b, p in ORDER:
        tasks[name](b, p)

    for i in range(2):
        value = own_end[i]
        for b in range(STEPS):
            if b != OWN:
                recv(back_in.at[b, i], b, 0, BACK + i)
                value = value + back_in[b, i].astype(F32)
        ends[i] = value.astype(BF16)

    for b in range(STEPS):
        for p in range(len(PARTS)):
            if p == 0:
                for i in range(3):
                    sent(core_out.at[b, i], b, p, CORE_SUM + i)
            if p == X_FIRST:
                kinds = (Y_FAR, Y_NEAR, Y_NEAR + 2, Y_GIVE, Y_GIVE + 2, Y_PASS)
                kinds += tuple(range(X_SUM_ALL, KINDS)) + tuple(range(CORE_GIVE, BACK))
            else:
                kinds = tuple(range(Y_FAR, BACK))
            for kind in kinds:
                sent(spot(b, piece(y, 0), wide(p, core)), b, p, kind)
        if b != OWN:
            for i in range(2):
                sent(back_out.at[b, i], b, 0, BACK + i)
                sent(rows.at[b, i], b, 0, FETCH + i)

    for b in range(STEPS):
        for store in stores(b):
            store.wait()


def exchange(n_row, n_col, tokens, gate_weight, up_weight, down_weight, cotangent):
    toks, feats = tokens.shape
    hidden = gate_weight.shape[1]
    half = hidden // 2
    n_y = n_col // 4
    pieces = n_col // 2
    span = toks // pieces
    any_space = pl.BlockSpec(memory_space=pl.ANY)
    vmem = pl.BlockSpec(memory_space=pltpu.VMEM)
    return pl.pallas_call(
        functools.partial(exchange_kernel, n_row, n_y),
        out_shape=(
            jax.ShapeDtypeStruct((2, toks, feats), BF16),
            jax.ShapeDtypeStruct((2, STEPS * toks, hidden), BF16),
            jax.ShapeDtypeStruct((STEPS, hidden + feats, toks), BF16),
            jax.ShapeDtypeStruct((STEPS * toks, feats), BF16),
        ),
        in_specs=[any_space] * 5,
        out_specs=(vmem, any_space, any_space, any_space),
        scratch_shapes=[
            pltpu.VMEM(gate_weight.shape, BF16),
            pltpu.VMEM(up_weight.shape, BF16),
            pltpu.VMEM(down_weight.shape, BF16),
            pltpu.VMEM((hidden, feats), BF16),
            pltpu.VMEM((hidden, feats), BF16),
            pltpu.VMEM((feats, hidden), BF16),
            pltpu.VMEM((STEPS, 2, toks, feats), BF16),
            pltpu.VMEM((STEPS, 3, pieces, span, half), F32),
            pltpu.VMEM((STEPS, 3, pieces, span, half), F32),
            pltpu.VMEM((STEPS, 3, pieces, span, half), F32),
            pltpu.VMEM((STEPS, 3, pieces, span, half), BF16),
            pltpu.VMEM((STEPS, 2, 3, span, half), BF16),
            pltpu.VMEM((STEPS, 2, 2, 3, span, half), BF16),
            pltpu.VMEM((STEPS, 3, span, half), BF16),
            pltpu.VMEM((STEPS, 3, span, half), BF16),
            pltpu.VMEM((STEPS, 3, n_y, span, PARTS[X_FIRST][1]), BF16),
            pltpu.VMEM((STEPS, 3, toks, hidden), BF16),
            pltpu.VMEM((2, toks, feats), F32),
            pltpu.VMEM((STEPS, 2, toks, feats), BF16),
            pltpu.VMEM((STEPS, 2, toks, feats), BF16),
            pltpu.VMEM((STEPS, feats, toks), BF16),
            pltpu.VMEM((STEPS, hidden, toks), BF16),
            pltpu.SemaphoreType.DMA((STEPS, len(PARTS), KINDS)),
            pltpu.SemaphoreType.DMA((STEPS, len(PARTS), KINDS)),
            pltpu.SemaphoreType.DMA((8,)),
            pltpu.SemaphoreType.DMA((STEPS, 4)),
        ],
        compiler_params=pltpu.CompilerParams(
            collective_id=0, has_side_effects=True, vmem_limit_bytes=60 * 2**20
        ),
        name="exchange",
    )(tokens, gate_weight, up_weight, down_weight, cotangent)


def weight_kernel(
    ends_hbm,
    acts_hbm,
    turned_hbm,
    cot_hbm,
    mixed_hbm,
    tokens_hbm,
    gate_hbm,
    up_hbm,
    down_hbm,
    acts,
    turned,
    cot,
    ends,
    x,
    gate,
    up,
    down,
    in_sem,
    out_sem,
    end_sem,
):
    hidden = acts.shape[-1]
    toks = turned.shape[-1]
    copy = pltpu.make_async_copy
    tiles = [pl.ds(at, min(TILE, hidden - at)) for at in range(0, hidden, TILE)]
    tail = pl.ds(hidden, x.shape[0])
    load_x = copy(turned_hbm.at[:, tail], turned.at[:, tail], end_sem.at[0])
    load_cot = copy(cot_hbm, cot, end_sem.at[1])
    load_ends = copy(ends_hbm, ends, end_sem.at[2])
    loads = [
        (
            copy(acts_hbm.at[0, :, at], acts.at[0, :, at], in_sem.at[i, 0]),
            copy(acts_hbm.at[1, :, at], acts.at[1, :, at], in_sem.at[i, 1]),
            copy(turned_hbm.at[:, at], turned.at[:, at], in_sem.at[i, 2]),
        )
        for i, at in enumerate(tiles)
    ]
    load_x.start()
    for i, group in enumerate(loads):
        for load in group:
            load.start()
        if i == 0:
            load_cot.start()
    load_ends.start()
    load_x.wait()
    for b in range(STEPS):
        x[:, b * toks : (b + 1) * toks] = turned[b, hidden:]
    stores = []

    def store(src, dst, sem):
        stores.append(copy(src, dst, sem))
        stores[-1].start()

    for i, at in enumerate(tiles):
        for k, (out, out_hbm) in enumerate(((gate, gate_hbm), (up, up_hbm))):
            loads[i][k].wait()
            out[:, at] = nn(x[...], acts[k, :, at]).astype(BF16)
            store(out.at[:, at], out_hbm.at[:, at], out_sem.at[i, k])
        if i == 0:
            load_cot.wait()
        loads[i][2].wait()
        h = jnp.concatenate([turned[b, at] for b in range(STEPS)], axis=1)
        down[at] = nn(h, cot[...]).astype(BF16)
        store(down.at[at], down_hbm.at[at], out_sem.at[i, 2])
        if i == 0:
            load_ends.wait()
            store(ends.at[0], mixed_hbm, end_sem.at[3])
            store(ends.at[1], tokens_hbm, end_sem.at[4])
    for out in stores:
        out.wait()


def weight_grads(ends, acts, turned, cot):
    _, toks, feats = ends.shape
    _, depth, hidden = acts.shape
    any_space = pl.BlockSpec(memory_space=pl.ANY)
    return pl.pallas_call(
        weight_kernel,
        out_shape=(
            jax.ShapeDtypeStruct((toks, feats), BF16),
            jax.ShapeDtypeStruct((toks, feats), BF16),
            jax.ShapeDtypeStruct((feats, hidden), BF16),
            jax.ShapeDtypeStruct((feats, hidden), BF16),
            jax.ShapeDtypeStruct((hidden, feats), BF16),
        ),
        in_specs=[any_space] * 4,
        out_specs=(any_space,) * 5,
        scratch_shapes=[
            pltpu.VMEM(acts.shape, BF16),
            pltpu.VMEM(turned.shape, BF16),
            pltpu.VMEM(cot.shape, BF16),
            pltpu.VMEM(ends.shape, BF16),
            pltpu.VMEM((feats, depth), BF16),
            pltpu.VMEM((feats, hidden), BF16),
            pltpu.VMEM((feats, hidden), BF16),
            pltpu.VMEM((hidden, feats), BF16),
            pltpu.SemaphoreType.DMA((pl.cdiv(hidden, TILE), 3)),
            pltpu.SemaphoreType.DMA((pl.cdiv(hidden, TILE), 3)),
            pltpu.SemaphoreType.DMA((5,)),
        ],
        compiler_params=pltpu.CompilerParams(vmem_limit_bytes=60 * 2**20),
        name="weight_grads",
    )(ends, acts, turned, cot)


def solution(mesh):
    n_row, n_col = mesh.shape["row"], mesh.shape["col"]
    placed = (P("row", "col"), P("col", "row"), P("col", "row"), P("row", "col"), P("row", "col"))

    def body(tokens, gate_weight, up_weight, down_weight, cotangent):
        return weight_grads(
            *exchange(n_row, n_col, tokens, gate_weight, up_weight, down_weight, cotangent)
        )

    return jax.shard_map(
        body,
        mesh=mesh,
        in_specs=placed,
        out_specs=(
            P("row", "col"),
            P("row", "col"),
            P("col", "row"),
            P("col", "row"),
            P("row", "col"),
        ),
        check_vma=False,
    )
```

```python
import functools

import jax
import jax.numpy as jnp
from jax import lax
from jax.experimental import pallas as pl
from jax.experimental.pallas import tpu as pltpu
from jax.sharding import PartitionSpec as P

MESH = pl.DeviceIdType.MESH
STEPS = 3
F32 = jnp.float32
BF16 = jnp.bfloat16

CORE_SUM = 0
Y_FAR = 3
Y_NEAR = 5
X_SUM = 9
X_GIVE = 10
Y_GIVE = 11
Y_PASS = 15
CORE_GIVE = 17
BACK = 25
FETCH = 27
X_SUM_ALL = 29
X_GIVE_ALL = 33
KINDS = 37

SHIFTS = (0, 2, 1)
PARTS = ((0, 640), (640, 256))
X_FIRST = len(PARTS) - 1
TILE = 896
ORDER = (
    ("second", 0, 0),
    ("first", 0, 0),
    ("third", 0, 0),
    ("chip_sum", 0, 0),
    ("chip_sum", 0, 1),
    ("arrive", 1, 0),
    ("flip", 0, 0),
    ("first", 1, 0),
    ("arrive", 1, 1),
    ("second", 1, 0),
    ("middle", 0, 0),
    ("turn", 1, 0),
    ("cross", 0, 1),
    ("third", 1, 0),
    ("chip_sum", 1, 0),
    ("chip_sum", 1, 1),
    ("arrive", 2, 0),
    ("first", 2, 0),
    ("middle", 0, 1),
    ("arrive", 2, 1),
    ("second", 2, 0),
    ("middle", 1, 0),
    ("cross", 0, 0),
    ("third", 2, 0),
    ("cross", 1, 1),
    ("chip_sum", 2, 0),
    ("chip_sum", 2, 1),
    ("cross", 1, 0),
    ("middle", 1, 1),
    ("middle", 2, 0),
    ("activate", 0, 1),
    ("activate", 0, 0),
    ("cross", 2, 1),
    ("cross", 2, 0),
    ("activate", 1, 1),
    ("activate", 1, 0),
    ("middle", 2, 1),
    ("activate", 2, 0),
    ("pass_on", 1, 1),
    ("activate", 2, 1),
    ("give_second", 1, 0),
    ("give_second", 2, 0),
    ("turn", 0, 0),
    ("flip", 2, 0),
    ("pass_up", 1, 0),
    ("pass_on", 2, 1),
    ("finish_on", 1, 1),
    ("pass_up", 2, 0),
    ("swap_own", 2, 1),
    ("pass_down", 1, 0),
    ("swap_near", 1, 1),
    ("pass_down", 2, 0),
    ("finish_on", 2, 1),
    ("swap_own", 1, 1),
    ("finish", 1, 0),
    ("pass_on", 0, 1),
    ("give_second", 0, 0),
    ("swap_far", 1, 1),
    ("flip", 1, 0),
    ("swap_near", 2, 1),
    ("swap_own", 0, 1),
    ("swap_far", 2, 1),
    ("turn", 2, 0),
    ("finish", 2, 0),
    ("outputs", 1, 0),
    ("finish_on", 0, 1),
    ("pass_up", 0, 0),
    ("outputs", 2, 0),
    ("pass_down", 0, 0),
    ("weights", 1, 0),
    ("swap_far", 0, 1),
    ("swap_near", 0, 1),
    ("finish", 0, 0),
    ("outputs", 0, 0),
    ("weights", 2, 0),
    ("weights", 0, 0),
)


OWN, ONE, TWO = (SHIFTS.index(shift) for shift in range(STEPS))


def nn(a, b):
    return lax.dot_general(a, b, (((1,), (0,)), ((), ())), preferred_element_type=F32)


def nt(a, b):
    return lax.dot_general(a, b, (((1,), (1,)), ((), ())), preferred_element_type=F32)


def tn(a, b):
    return lax.dot_general(a, b, (((0,), (0,)), ((), ())), preferred_element_type=F32)


def exchange_kernel(
    n_row,
    n_y,
    tok,
    wg_hbm,
    wu_hbm,
    wd_hbm,
    cot,
    ends,
    acts_hbm,
    turned_hbm,
    cot_hbm,
    wg,
    wu,
    wd,
    wg_flip,
    wu_flip,
    wd_flip,
    rows,
    core_out,
    core_in,
    total,
    total16,
    far_in,
    near_in,
    x_out,
    x_in,
    x_all,
    acts,
    own_end,
    back_out,
    back_in,
    turned_x,
    turned_h,
    send_sem,
    recv_sem,
    local_sem,
    out_sem,
):
    r = lax.axis_index("row")
    c = lax.axis_index("col")
    core = lax.rem(c, 2)
    xl = lax.rem(c // 2, 2)
    y = c // 4
    half = total.shape[-1]
    toks = rows.shape[2]
    span = far_in.shape[-2]

    def col(yy, xx, cc):
        return (yy * 2 + xx) * 2 + cc

    y_up = lax.rem(y + 1, n_y)
    y_down = lax.rem(y + n_y - 1, n_y)
    y_opp = lax.rem(y + 2, n_y)
    to_core = (r, col(y, xl, 1 - core))
    to_x = (r, col(y, 1 - xl, core))
    to_up = (r, col(y_up, xl, core))
    to_down = (r, col(y_down, xl, core))

    y_on = lax.rem(y + 1 + 2 * core, n_y)
    y_off = lax.rem(y + 3 + 2 * core, n_y)
    to_on = (r, col(y_on, xl, core))
    to_off = (r, col(y_off, xl, core))
    chunks = (y, y_up, y_opp, y_down)

    def to_row(by):
        return (lax.rem(r + n_row + by, n_row), c)

    def piece(yy, which):
        return yy * 2 + (xl if which == 0 else 1 - xl)

    def copy(src, dst, b, p, kind, device):
        return pltpu.make_async_remote_copy(
            src_ref=src,
            dst_ref=dst,
            send_sem=send_sem.at[b, p, kind],
            recv_sem=recv_sem.at[b, p, kind],
            device_id=device,
            device_id_type=MESH,
        )

    def recv(dst, b, p, kind):
        copy(dst, dst, b, p, kind, to_core).wait_recv()

    def sent(src, b, p, kind):
        copy(src, src, b, p, kind, to_core).wait_send()

    def half_of(which):
        return pl.ds(pl.multiple_of(which * half, 128), half)

    mine, other = half_of(core), half_of(1 - core)

    loads = {}

    def load(name, src, dst):
        loads[name] = pltpu.make_async_copy(src, dst, local_sem.at[len(loads)])
        loads[name].start()

    def loaded(*names):
        for name in names:
            if name in loads:
                loads.pop(name).wait()

    load("x", tok, rows.at[OWN, 0])
    load("gate_other", wg_hbm.at[:, other], wg.at[:, other])
    load("up_other", wu_hbm.at[:, other], wu.at[:, other])
    load("dy", cot, rows.at[OWN, 1])
    load("down_other", wd_hbm.at[other], wd.at[other])
    load("gate_mine", wg_hbm.at[:, mine], wg.at[:, mine])
    load("up_mine", wu_hbm.at[:, mine], wu.at[:, mine])
    load("down_mine", wd_hbm.at[mine], wd.at[mine])

    barrier = pltpu.get_barrier_semaphore()
    partners = [to_core, to_x, to_up, to_down] + [to_row(by) for by in (1, 2, -1, -2)]
    for partner in partners:
        pl.semaphore_signal(barrier, inc=1, device_id=partner, device_id_type=MESH)
    pl.semaphore_wait(barrier, len(partners))

    first_of_pair = lax.rem(r, 2) == 0
    for i, src in enumerate((tok, cot)):
        copy(src, rows.at[TWO, i], TWO, 0, FETCH + i, to_row(2)).start()

    @pl.when(first_of_pair)
    def _():
        for i, src in enumerate((tok, cot)):
            copy(src, rows.at[ONE, i], ONE, 0, FETCH + i, to_row(1)).start()

    def arrive(b, i):
        recv(rows.at[b, i], b, 0, FETCH + i)
        if b == TWO:

            @pl.when(jnp.logical_not(first_of_pair))
            def _():
                copy(rows.at[b, i], rows.at[ONE, i], ONE, 0, FETCH + i, to_row(-1)).start()

    def lanes(p):
        return pl.ds(*PARTS[p])

    def wide(p, which):
        off, size = PARTS[p]
        return pl.ds(pl.multiple_of(which * half + off, 128), size)

    flipped = set()

    def flip(which, p):
        if which == 0:
            loaded("down_other", "down_mine")
            wd_flip[...] = wd[...].T
        elif which == 1:
            loaded("gate_other", "gate_mine")
            wg_flip[...] = wg[...].T
        else:
            loaded("up_other", "up_mine")
            wu_flip[...] = wu[...].T
        flipped.add(which)

    def product(b, i, where):
        if i < 2:
            part = nn(rows[b, 0], (wg, wu)[i][:, where])
        elif 0 in flipped:
            part = nn(rows[b, 1], wd_flip[:, where])
        else:
            part = nt(rows[b, 1], wd[where, :])
        return part.reshape(total.shape[2:])

    def give_core(b, arrays):
        for i in arrays:
            core_out[b, i] = product(b, i, other)
            copy(core_out.at[b, i], core_in.at[b, i], b, 0, CORE_SUM + i, to_core).start()

    def first(b, p):
        loaded("x", "gate_other", "up_other")
        give_core(b, (0, 1))

    def second(b, p):
        loaded("dy", "down_other")
        give_core(b, (2,))

    def third(b, p):
        loaded("gate_mine", "up_mine", "down_mine")
        for i in range(3):
            total[b, i] = product(b, i, mine)

    summed = set()

    def chip_sum(b, p):
        for i in range(3):
            if b not in summed:
                recv(core_in.at[b, i], b, 0, CORE_SUM + i)
            value = total[b, i, :, :, lanes(p)] + core_in[b, i, :, :, lanes(p)]
            total[b, i, :, :, lanes(p)] = value
            total16[b, i, :, :, lanes(p)] = value.astype(BF16)
        summed.add(b)
        if p == X_FIRST:
            for k, yy in enumerate(chunks):
                copy(
                    total16.at[b, :, piece(yy, 1), :, lanes(p)],
                    x_all.at[b, :, yy],
                    b, p, X_SUM_ALL + k, to_x,
                ).start()
            return
        for way, (device, which) in enumerate(((to_up, 0), (to_down, 1))):
            copy(
                total16.at[b, :, piece(y_opp, which), :, lanes(p)],
                far_in.at[b, way, :, :, lanes(p)],
                b, p, Y_FAR + way, device,
            ).start()
        for way, (device, yy, which) in enumerate(((to_up, y_up, 1), (to_down, y_down, 0))):
            near(b, p, way, which, piece(yy, which), device)

    def near(b, p, way, which, at, device):
        copy(
            total16.at[b, :, at, :, lanes(p)],
            near_in.at[b, way, which, :, :, lanes(p)],
            b, p, Y_NEAR + way * 2 + which, device,
        ).start()

    def middle(b, p):
        if p == X_FIRST:
            recv(far_in.at[b, 0, :, :, lanes(p)], b, p, Y_FAR)
            at = piece(y_on, 0)
            value = total[b, :, at, :, lanes(p)] + far_in[b, 0, :, :, lanes(p)].astype(F32)
            total16[b, :, at, :, lanes(p)] = value.astype(BF16)
            near(b, p, 0, 0, at, to_on)
            return
        for way, (device, yy, which) in enumerate(((to_up, y_up, 0), (to_down, y_down, 1))):
            recv(far_in.at[b, way, :, :, lanes(p)], b, p, Y_FAR + way)
            at = piece(yy, which)
            value = total[b, :, at, :, lanes(p)] + far_in[b, way, :, :, lanes(p)].astype(F32)
            total16[b, :, at, :, lanes(p)] = value.astype(BF16)
            near(b, p, way, which, at, device)

    def y_sum(b, p, which):
        for way in range(2):
            recv(near_in.at[b, way, which, :, :, lanes(p)], b, p, Y_NEAR + way * 2 + which)
        return total[b, :, piece(y, which), :, lanes(p)] + (
            near_in[b, 0, which, :, :, lanes(p)].astype(F32)
            + near_in[b, 1, which, :, :, lanes(p)].astype(F32)
        )

    def cross(b, p):
        if p == X_FIRST:
            for k, yy in enumerate(chunks):
                recv(x_all.at[b, :, yy], b, p, X_SUM_ALL + k)
                at = piece(yy, 0)
                value = total[b, :, at, :, lanes(p)] + x_all[b, :, yy].astype(F32)
                total[b, :, at, :, lanes(p)] = value
                if k != 0:
                    total16[b, :, at, :, lanes(p)] = value.astype(BF16)
            copy(
                total16.at[b, :, piece(y_opp, 0), :, lanes(p)],
                far_in.at[b, 0, :, :, lanes(p)],
                b, p, Y_FAR, to_on,
            ).start()
            near(b, p, 1, 0, piece(y_off, 0), to_off)
            return
        x_out[b, :, :, lanes(p)] = y_sum(b, p, 1).astype(x_out.dtype)
        copy(
            x_out.at[b, :, :, lanes(p)], x_in.at[b, :, :, lanes(p)], b, p, X_SUM, to_x
        ).start()

    def spot(b, at, where):
        return acts.at[b, :, pl.ds(pl.multiple_of(at * span, span), span), where]

    def give(b, p, yy, which, kind, device):
        ref = spot(b, piece(yy, which), wide(p, core))
        copy(ref, ref, b, p, kind, device).start()

    def take(b, p, yy, which, kind, side):
        recv(spot(b, piece(yy, which), wide(p, side)), b, p, kind)

    def activate(b, p):
        value = y_sum(b, p, 0)
        if p != X_FIRST:
            recv(x_in.at[b, :, :, lanes(p)], b, p, X_SUM)
            value = value + x_in[b, :, :, lanes(p)].astype(F32)
        gate, up, grad_hidden = value[0], value[1], value[2]
        sig = jax.nn.sigmoid(gate)
        act = gate * sig
        at = pl.ds(pl.multiple_of(piece(y, 0) * span, span), span)
        where = wide(p, core)
        acts[b, 0, at, where] = (act * up).astype(BF16)
        acts[b, 1, at, where] = (grad_hidden * up * sig * (1.0 + gate * (1.0 - sig))).astype(BF16)
        acts[b, 2, at, where] = (grad_hidden * act).astype(BF16)
        give(b, p, y, 0, X_GIVE_ALL if p == X_FIRST else X_GIVE, to_x)
        give(b, p, y, 0, Y_GIVE, to_up)
        give(b, p, y, 0, Y_GIVE + 2, to_down)
        give(b, p, y, 0, CORE_GIVE, to_core)

    def give_second(b, p):
        take(b, p, y, 1, X_GIVE, core)
        give(b, p, y, 1, Y_GIVE + 1, to_up)
        give(b, p, y, 1, Y_GIVE + 3, to_down)
        give(b, p, y, 1, CORE_GIVE + 1, to_core)

    def swap(b, p, ks):
        for k in ks:
            take(b, p, chunks[k], 1, X_GIVE_ALL + k, core)
            give(b, p, chunks[k], 1, CORE_GIVE + 2 * k + 1, to_core)

    def swap_own(b, p):
        swap(b, p, (0,))

    def swap_near(b, p):
        swap(b, p, (1, 3))

    def swap_far(b, p):
        swap(b, p, (2,))

    def pass_on(b, p):
        take(b, p, y_down, 0, Y_GIVE, core)
        take(b, p, y_up, 0, Y_GIVE + 2, core)
        give(b, p, y_off, 0, Y_PASS, to_on)
        for k in (1, 3):
            give(b, p, chunks[k], 0, X_GIVE_ALL + k, to_x)
            give(b, p, chunks[k], 0, CORE_GIVE + 2 * k, to_core)

    def finish_on(b, p):
        take(b, p, y_opp, 0, Y_PASS, core)
        give(b, p, y_opp, 0, X_GIVE_ALL + 2, to_x)
        give(b, p, y_opp, 0, CORE_GIVE + 4, to_core)

    def pass_up(b, p):
        take(b, p, y_down, 0, Y_GIVE, core)
        give(b, p, y_down, 0, Y_PASS, to_up)
        give(b, p, y_down, 0, CORE_GIVE + 6, to_core)
        take(b, p, y_up, 0, Y_GIVE + 2, core)
        give(b, p, y_up, 0, CORE_GIVE + 2, to_core)

    def pass_down(b, p):
        take(b, p, y_up, 1, Y_GIVE + 3, core)
        give(b, p, y_up, 1, Y_PASS + 1, to_down)
        give(b, p, y_up, 1, CORE_GIVE + 3, to_core)
        take(b, p, y_down, 1, Y_GIVE + 1, core)
        give(b, p, y_down, 1, CORE_GIVE + 7, to_core)

    def finish(b, p):
        for which in range(2):
            take(b, p, y_opp, which, Y_PASS + which, core)
            give(b, p, y_opp, which, CORE_GIVE + 4 + which, to_core)

    def outputs(b, p):
        for p in range(len(PARTS)):
            for k, yy in enumerate((y, y_up, y_opp, y_down)):
                for which in range(2):
                    take(b, p, yy, which, CORE_GIVE + 2 * k + which, 1 - core)
        for i in range(2):
            if i == 0:
                value = nn(acts[b, 0], wd[...])
            else:
                value = nn(acts[b, 1], wg_flip[...]) + nn(acts[b, 2], wu_flip[...])
            if b == OWN:
                own_end[i] = value
            else:
                back_out[b, i] = value.astype(BF16)
                copy(
                    back_out.at[b, i], back_in.at[b, i], b, 0, BACK + i, to_row(-SHIFTS[b])
                ).start()

    def stores(b):
        at = pl.ds(b * toks, toks)
        hidden = turned_h.shape[1]
        return tuple(
            pltpu.make_async_copy(src, dst, out_sem.at[b, i])
            for i, (src, dst) in enumerate(
                (
                    (acts.at[b, pl.ds(1, 2)], acts_hbm.at[:, at]),
                    (turned_h.at[b], turned_hbm.at[b, pl.ds(0, hidden)]),
                    (turned_x.at[b], turned_hbm.at[b, pl.ds(hidden, turned_x.shape[1])]),
                    (rows.at[b, 1], cot_hbm.at[at]),
                )
            )
        )

    def turn(b, p):
        turned_x[b] = rows[b, 0].T

    def weights(b, p):
        at_once, after_turn, *rest = stores(b)
        at_once.start()
        for store in rest:
            store.start()
        turned_h[b] = acts[b, 0].T
        after_turn.start()

    tasks = dict(
        flip=flip,
        arrive=arrive,
        first=first,
        second=second,
        third=third,
        chip_sum=chip_sum,
        middle=middle,
        cross=cross,
        activate=activate,
        give_second=give_second,
        swap_own=swap_own,
        swap_near=swap_near,
        swap_far=swap_far,
        pass_on=pass_on,
        finish_on=finish_on,
        pass_up=pass_up,
        pass_down=pass_down,
        finish=finish,
        outputs=outputs,
        turn=turn,
        weights=weights,
    )
    for name, b, p in ORDER:
        tasks[name](b, p)

    for i in range(2):
        value = own_end[i]
        for b in range(STEPS):
            if b != OWN:
                recv(back_in.at[b, i], b, 0, BACK + i)
                value = value + back_in[b, i].astype(F32)
        ends[i] = value.astype(BF16)

    for b in range(STEPS):
        for p in range(len(PARTS)):
            if p == 0:
                for i in range(3):
                    sent(core_out.at[b, i], b, p, CORE_SUM + i)
            if p == X_FIRST:
                kinds = (Y_FAR, Y_NEAR, Y_NEAR + 2, Y_GIVE, Y_GIVE + 2, Y_PASS)
                kinds += tuple(range(X_SUM_ALL, KINDS)) + tuple(range(CORE_GIVE, BACK))
            else:
                kinds = tuple(range(Y_FAR, BACK))
            for kind in kinds:
                sent(spot(b, piece(y, 0), wide(p, core)), b, p, kind)
        if b != OWN:
            for i in range(2):
                sent(back_out.at[b, i], b, 0, BACK + i)
                sent(rows.at[b, i], b, 0, FETCH + i)

    for b in range(STEPS):
        for store in stores(b):
            store.wait()


def exchange(n_row, n_col, tokens, gate_weight, up_weight, down_weight, cotangent):
    toks, feats = tokens.shape
    hidden = gate_weight.shape[1]
    half = hidden // 2
    n_y = n_col // 4
    pieces = n_col // 2
    span = toks // pieces
    any_space = pl.BlockSpec(memory_space=pl.ANY)
    vmem = pl.BlockSpec(memory_space=pltpu.VMEM)
    return pl.pallas_call(
        functools.partial(exchange_kernel, n_row, n_y),
        out_shape=(
            jax.ShapeDtypeStruct((2, toks, feats), BF16),
            jax.ShapeDtypeStruct((2, STEPS * toks, hidden), BF16),
            jax.ShapeDtypeStruct((STEPS, hidden + feats, toks), BF16),
            jax.ShapeDtypeStruct((STEPS * toks, feats), BF16),
        ),
        in_specs=[any_space] * 5,
        out_specs=(vmem, any_space, any_space, any_space),
        scratch_shapes=[
            pltpu.VMEM(gate_weight.shape, BF16),
            pltpu.VMEM(up_weight.shape, BF16),
            pltpu.VMEM(down_weight.shape, BF16),
            pltpu.VMEM((hidden, feats), BF16),
            pltpu.VMEM((hidden, feats), BF16),
            pltpu.VMEM((feats, hidden), BF16),
            pltpu.VMEM((STEPS, 2, toks, feats), BF16),
            pltpu.VMEM((STEPS, 3, pieces, span, half), F32),
            pltpu.VMEM((STEPS, 3, pieces, span, half), F32),
            pltpu.VMEM((STEPS, 3, pieces, span, half), F32),
            pltpu.VMEM((STEPS, 3, pieces, span, half), BF16),
            pltpu.VMEM((STEPS, 2, 3, span, half), BF16),
            pltpu.VMEM((STEPS, 2, 2, 3, span, half), BF16),
            pltpu.VMEM((STEPS, 3, span, half), BF16),
            pltpu.VMEM((STEPS, 3, span, half), BF16),
            pltpu.VMEM((STEPS, 3, n_y, span, PARTS[X_FIRST][1]), BF16),
            pltpu.VMEM((STEPS, 3, toks, hidden), BF16),
            pltpu.VMEM((2, toks, feats), F32),
            pltpu.VMEM((STEPS, 2, toks, feats), BF16),
            pltpu.VMEM((STEPS, 2, toks, feats), BF16),
            pltpu.VMEM((STEPS, feats, toks), BF16),
            pltpu.VMEM((STEPS, hidden, toks), BF16),
            pltpu.SemaphoreType.DMA((STEPS, len(PARTS), KINDS)),
            pltpu.SemaphoreType.DMA((STEPS, len(PARTS), KINDS)),
            pltpu.SemaphoreType.DMA((8,)),
            pltpu.SemaphoreType.DMA((STEPS, 4)),
        ],
        compiler_params=pltpu.CompilerParams(
            collective_id=0, has_side_effects=True, vmem_limit_bytes=60 * 2**20
        ),
        name="exchange",
    )(tokens, gate_weight, up_weight, down_weight, cotangent)


def weight_kernel(
    ends_hbm,
    acts_hbm,
    turned_hbm,
    cot_hbm,
    mixed_hbm,
    tokens_hbm,
    gate_hbm,
    up_hbm,
    down_hbm,
    acts,
    turned,
    cot,
    ends,
    x,
    gate,
    up,
    down,
    in_sem,
    out_sem,
    end_sem,
):
    hidden = acts.shape[-1]
    toks = turned.shape[-1]
    copy = pltpu.make_async_copy
    tiles = [pl.ds(at, min(TILE, hidden - at)) for at in range(0, hidden, TILE)]
    tail = pl.ds(hidden, x.shape[0])
    load_x = copy(turned_hbm.at[:, tail], turned.at[:, tail], end_sem.at[0])
    load_cot = copy(cot_hbm, cot, end_sem.at[1])
    load_ends = copy(ends_hbm, ends, end_sem.at[2])
    loads = [
        (
            copy(acts_hbm.at[0, :, at], acts.at[0, :, at], in_sem.at[i, 0]),
            copy(acts_hbm.at[1, :, at], acts.at[1, :, at], in_sem.at[i, 1]),
            copy(turned_hbm.at[:, at], turned.at[:, at], in_sem.at[i, 2]),
        )
        for i, at in enumerate(tiles)
    ]
    load_x.start()
    for i, group in enumerate(loads):
        for load in group:
            load.start()
        if i == 0:
            load_cot.start()
    load_ends.start()
    load_x.wait()
    for b in range(STEPS):
        x[:, b * toks : (b + 1) * toks] = turned[b, hidden:]
    stores = []

    def store(src, dst, sem):
        stores.append(copy(src, dst, sem))
        stores[-1].start()

    for i, at in enumerate(tiles):
        for k, (out, out_hbm) in enumerate(((gate, gate_hbm), (up, up_hbm))):
            loads[i][k].wait()
            out[:, at] = nn(x[...], acts[k, :, at]).astype(BF16)
            store(out.at[:, at], out_hbm.at[:, at], out_sem.at[i, k])
        if i == 0:
            load_cot.wait()
        loads[i][2].wait()
        h = jnp.concatenate([turned[b, at] for b in range(STEPS)], axis=1)
        down[at] = nn(h, cot[...]).astype(BF16)
        store(down.at[at], down_hbm.at[at], out_sem.at[i, 2])
        if i == 0:
            load_ends.wait()
            store(ends.at[0], mixed_hbm, end_sem.at[3])
            store(ends.at[1], tokens_hbm, end_sem.at[4])
    for out in stores:
        out.wait()


def weight_grads(ends, acts, turned, cot):
    _, toks, feats = ends.shape
    _, depth, hidden = acts.shape
    any_space = pl.BlockSpec(memory_space=pl.ANY)
    return pl.pallas_call(
        weight_kernel,
        out_shape=(
            jax.ShapeDtypeStruct((toks, feats), BF16),
            jax.ShapeDtypeStruct((toks, feats), BF16),
            jax.ShapeDtypeStruct((feats, hidden), BF16),
            jax.ShapeDtypeStruct((feats, hidden), BF16),
            jax.ShapeDtypeStruct((hidden, feats), BF16),
        ),
        in_specs=[any_space] * 4,
        out_specs=(any_space,) * 5,
        scratch_shapes=[
            pltpu.VMEM(acts.shape, BF16),
            pltpu.VMEM(turned.shape, BF16),
            pltpu.VMEM(cot.shape, BF16),
            pltpu.VMEM(ends.shape, BF16),
            pltpu.VMEM((feats, depth), BF16),
            pltpu.VMEM((feats, hidden), BF16),
            pltpu.VMEM((feats, hidden), BF16),
            pltpu.VMEM((hidden, feats), BF16),
            pltpu.SemaphoreType.DMA((pl.cdiv(hidden, TILE), 3)),
            pltpu.SemaphoreType.DMA((pl.cdiv(hidden, TILE), 3)),
            pltpu.SemaphoreType.DMA((5,)),
        ],
        compiler_params=pltpu.CompilerParams(vmem_limit_bytes=60 * 2**20),
        name="weight_grads",
    )(ends, acts, turned, cot)


def solution(mesh):
    n_row, n_col = mesh.shape["row"], mesh.shape["col"]
    placed = (P("row", "col"), P("col", "row"), P("col", "row"), P("row", "col"), P("row", "col"))

    def body(tokens, gate_weight, up_weight, down_weight, cotangent):
        return weight_grads(
            *exchange(n_row, n_col, tokens, gate_weight, up_weight, down_weight, cotangent)
        )

    return jax.shard_map(
        body,
        mesh=mesh,
        in_specs=placed,
        out_specs=(
            P("row", "col"),
            P("row", "col"),
            P("col", "row"),
            P("col", "row"),
            P("row", "col"),
        ),
        check_vma=False,
    )
```

```python
import functools

import jax
import jax.numpy as jnp
from jax import lax
from jax.experimental import pallas as pl
from jax.experimental.pallas import tpu as pltpu
from jax.sharding import PartitionSpec as P

MESH = pl.DeviceIdType.MESH
STEPS = 3
F32 = jnp.float32
BF16 = jnp.bfloat16

CORE_SUM = 0
Y_FAR = 3
Y_NEAR = 5
X_SUM = 9
X_GIVE = 10
Y_GIVE = 11
Y_PASS = 15
CORE_GIVE = 17
BACK = 25
FETCH = 27
X_SUM_ALL = 29
X_GIVE_ALL = 33
KINDS = 37

SHIFTS = (0, 2, 1)
PARTS = ((0, 640), (640, 256))
X_FIRST = len(PARTS) - 1
TILE = 896
ORDER = (
    ("second", 0, 0),
    ("first", 0, 0),
    ("third", 0, 0),
    ("chip_sum", 0, 0),
    ("chip_sum", 0, 1),
    ("arrive", 1, 0),
    ("flip", 0, 0),
    ("first", 1, 0),
    ("arrive", 1, 1),
    ("second", 1, 0),
    ("middle", 0, 0),
    ("turn", 1, 0),
    ("cross", 0, 1),
    ("third", 1, 0),
    ("chip_sum", 1, 0),
    ("chip_sum", 1, 1),
    ("arrive", 2, 0),
    ("first", 2, 0),
    ("middle", 0, 1),
    ("arrive", 2, 1),
    ("second", 2, 0),
    ("middle", 1, 0),
    ("cross", 0, 0),
    ("third", 2, 0),
    ("cross", 1, 1),
    ("chip_sum", 2, 0),
    ("chip_sum", 2, 1),
    ("cross", 1, 0),
    ("middle", 1, 1),
    ("middle", 2, 0),
    ("activate", 0, 1),
    ("activate", 0, 0),
    ("cross", 2, 1),
    ("cross", 2, 0),
    ("activate", 1, 1),
    ("activate", 1, 0),
    ("middle", 2, 1),
    ("activate", 2, 0),
    ("pass_on", 1, 1),
    ("activate", 2, 1),
    ("give_second", 1, 0),
    ("give_second", 2, 0),
    ("turn", 0, 0),
    ("flip", 2, 0),
    ("pass_up", 1, 0),
    ("pass_on", 2, 1),
    ("finish_on", 1, 1),
    ("pass_up", 2, 0),
    ("swap_own", 2, 1),
    ("pass_down", 1, 0),
    ("swap_near", 1, 1),
    ("pass_down", 2, 0),
    ("finish_on", 2, 1),
    ("swap_own", 1, 1),
    ("finish", 1, 0),
    ("pass_on", 0, 1),
    ("give_second", 0, 0),
    ("swap_far", 1, 1),
    ("flip", 1, 0),
    ("swap_near", 2, 1),
    ("swap_own", 0, 1),
    ("swap_far", 2, 1),
    ("turn", 2, 0),
    ("finish", 2, 0),
    ("outputs", 1, 0),
    ("finish_on", 0, 1),
    ("pass_up", 0, 0),
    ("outputs", 2, 0),
    ("pass_down", 0, 0),
    ("weights", 1, 0),
    ("swap_far", 0, 1),
    ("swap_near", 0, 1),
    ("finish", 0, 0),
    ("outputs", 0, 0),
    ("weights", 2, 0),
    ("weights", 0, 0),
)


OWN, ONE, TWO = (SHIFTS.index(shift) for shift in range(STEPS))


def nn(a, b):
    return lax.dot_general(a, b, (((1,), (0,)), ((), ())), preferred_element_type=F32)


def nt(a, b):
    return lax.dot_general(a, b, (((1,), (1,)), ((), ())), preferred_element_type=F32)


def tn(a, b):
    return lax.dot_general(a, b, (((0,), (0,)), ((), ())), preferred_element_type=F32)


def exchange_kernel(
    n_row,
    n_y,
    tok,
    wg_hbm,
    wu_hbm,
    wd_hbm,
    cot,
    ends,
    acts_hbm,
    turned_hbm,
    cot_hbm,
    wg,
    wu,
    wd,
    wg_flip,
    wu_flip,
    wd_flip,
    rows,
    core_out,
    core_in,
    total,
    total16,
    far_in,
    near_in,
    x_out,
    x_in,
    x_all,
    acts,
    own_end,
    back_out,
    back_in,
    turned_x,
    turned_h,
    send_sem,
    recv_sem,
    local_sem,
    out_sem,
):
    r = lax.axis_index("row")
    c = lax.axis_index("col")
    core = lax.rem(c, 2)
    xl = lax.rem(c // 2, 2)
    y = c // 4
    half = total.shape[-1]
    toks = rows.shape[2]
    span = far_in.shape[-2]

    def col(yy, xx, cc):
        return (yy * 2 + xx) * 2 + cc

    y_up = lax.rem(y + 1, n_y)
    y_down = lax.rem(y + n_y - 1, n_y)
    y_opp = lax.rem(y + 2, n_y)
    to_core = (r, col(y, xl, 1 - core))
    to_x = (r, col(y, 1 - xl, core))
    to_up = (r, col(y_up, xl, core))
    to_down = (r, col(y_down, xl, core))

    y_on = lax.rem(y + 1 + 2 * core, n_y)
    y_off = lax.rem(y + 3 + 2 * core, n_y)
    to_on = (r, col(y_on, xl, core))
    to_off = (r, col(y_off, xl, core))
    chunks = (y, y_up, y_opp, y_down)

    def to_row(by):
        return (lax.rem(r + n_row + by, n_row), c)

    def piece(yy, which):
        return yy * 2 + (xl if which == 0 else 1 - xl)

    def copy(src, dst, b, p, kind, device):
        return pltpu.make_async_remote_copy(
            src_ref=src,
            dst_ref=dst,
            send_sem=send_sem.at[b, p, kind],
            recv_sem=recv_sem.at[b, p, kind],
            device_id=device,
            device_id_type=MESH,
        )

    def recv(dst, b, p, kind):
        copy(dst, dst, b, p, kind, to_core).wait_recv()

    def sent(src, b, p, kind):
        copy(src, src, b, p, kind, to_core).wait_send()

    def half_of(which):
        return pl.ds(pl.multiple_of(which * half, 128), half)

    mine, other = half_of(core), half_of(1 - core)

    loads = {}

    def load(name, src, dst):
        loads[name] = pltpu.make_async_copy(src, dst, local_sem.at[len(loads)])
        loads[name].start()

    def loaded(*names):
        for name in names:
            if name in loads:
                loads.pop(name).wait()

    load("x", tok, rows.at[OWN, 0])
    load("gate_other", wg_hbm.at[:, other], wg.at[:, other])
    load("up_other", wu_hbm.at[:, other], wu.at[:, other])
    load("dy", cot, rows.at[OWN, 1])
    load("down_other", wd_hbm.at[other], wd.at[other])
    load("gate_mine", wg_hbm.at[:, mine], wg.at[:, mine])
    load("up_mine", wu_hbm.at[:, mine], wu.at[:, mine])
    load("down_mine", wd_hbm.at[mine], wd.at[mine])

    barrier = pltpu.get_barrier_semaphore()
    partners = [to_core, to_x, to_up, to_down] + [to_row(by) for by in (1, 2, -1, -2)]
    for partner in partners:
        pl.semaphore_signal(barrier, inc=1, device_id=partner, device_id_type=MESH)
    pl.semaphore_wait(barrier, len(partners))

    first_of_pair = lax.rem(r, 2) == 0
    for i, src in enumerate((tok, cot)):
        copy(src, rows.at[TWO, i], TWO, 0, FETCH + i, to_row(2)).start()

    @pl.when(first_of_pair)
    def _():
        for i, src in enumerate((tok, cot)):
            copy(src, rows.at[ONE, i], ONE, 0, FETCH + i, to_row(1)).start()

    def arrive(b, i):
        recv(rows.at[b, i], b, 0, FETCH + i)
        if b == TWO:

            @pl.when(jnp.logical_not(first_of_pair))
            def _():
                copy(rows.at[b, i], rows.at[ONE, i], ONE, 0, FETCH + i, to_row(-1)).start()

    def lanes(p):
        return pl.ds(*PARTS[p])

    def wide(p, which):
        off, size = PARTS[p]
        return pl.ds(pl.multiple_of(which * half + off, 128), size)

    flipped = set()

    def flip(which, p):
        if which == 0:
            loaded("down_other", "down_mine")
            wd_flip[...] = wd[...].T
        elif which == 1:
            loaded("gate_other", "gate_mine")
            wg_flip[...] = wg[...].T
        else:
            loaded("up_other", "up_mine")
            wu_flip[...] = wu[...].T
        flipped.add(which)

    def product(b, i, where):
        if i < 2:
            part = nn(rows[b, 0], (wg, wu)[i][:, where])
        elif 0 in flipped:
            part = nn(rows[b, 1], wd_flip[:, where])
        else:
            part = nt(rows[b, 1], wd[where, :])
        return part.reshape(total.shape[2:])

    def give_core(b, arrays):
        for i in arrays:
            core_out[b, i] = product(b, i, other)
            copy(core_out.at[b, i], core_in.at[b, i], b, 0, CORE_SUM + i, to_core).start()

    def first(b, p):
        loaded("x", "gate_other", "up_other")
        give_core(b, (0, 1))

    def second(b, p):
        loaded("dy", "down_other")
        give_core(b, (2,))

    def third(b, p):
        loaded("gate_mine", "up_mine", "down_mine")
        for i in range(3):
            total[b, i] = product(b, i, mine)

    summed = set()

    def chip_sum(b, p):
        for i in range(3):
            if b not in summed:
                recv(core_in.at[b, i], b, 0, CORE_SUM + i)
            value = total[b, i, :, :, lanes(p)] + core_in[b, i, :, :, lanes(p)]
            total[b, i, :, :, lanes(p)] = value
            total16[b, i, :, :, lanes(p)] = value.astype(BF16)
        summed.add(b)
        if p == X_FIRST:
            for k, yy in enumerate(chunks):
                copy(
                    total16.at[b, :, piece(yy, 1), :, lanes(p)],
                    x_all.at[b, :, yy],
                    b, p, X_SUM_ALL + k, to_x,
                ).start()
            return
        for way, (device, which) in enumerate(((to_up, 0), (to_down, 1))):
            copy(
                total16.at[b, :, piece(y_opp, which), :, lanes(p)],
                far_in.at[b, way, :, :, lanes(p)],
                b, p, Y_FAR + way, device,
            ).start()
        for way, (device, yy, which) in enumerate(((to_up, y_up, 1), (to_down, y_down, 0))):
            near(b, p, way, which, piece(yy, which), device)

    def near(b, p, way, which, at, device):
        copy(
            total16.at[b, :, at, :, lanes(p)],
            near_in.at[b, way, which, :, :, lanes(p)],
            b, p, Y_NEAR + way * 2 + which, device,
        ).start()

    def middle(b, p):
        if p == X_FIRST:
            recv(far_in.at[b, 0, :, :, lanes(p)], b, p, Y_FAR)
            at = piece(y_on, 0)
            value = total[b, :, at, :, lanes(p)] + far_in[b, 0, :, :, lanes(p)].astype(F32)
            total16[b, :, at, :, lanes(p)] = value.astype(BF16)
            near(b, p, 0, 0, at, to_on)
            return
        for way, (device, yy, which) in enumerate(((to_up, y_up, 0), (to_down, y_down, 1))):
            recv(far_in.at[b, way, :, :, lanes(p)], b, p, Y_FAR + way)
            at = piece(yy, which)
            value = total[b, :, at, :, lanes(p)] + far_in[b, way, :, :, lanes(p)].astype(F32)
            total16[b, :, at, :, lanes(p)] = value.astype(BF16)
            near(b, p, way, which, at, device)

    def y_sum(b, p, which):
        for way in range(2):
            recv(near_in.at[b, way, which, :, :, lanes(p)], b, p, Y_NEAR + way * 2 + which)
        return total[b, :, piece(y, which), :, lanes(p)] + (
            near_in[b, 0, which, :, :, lanes(p)].astype(F32)
            + near_in[b, 1, which, :, :, lanes(p)].astype(F32)
        )

    def cross(b, p):
        if p == X_FIRST:
            for k, yy in enumerate(chunks):
                recv(x_all.at[b, :, yy], b, p, X_SUM_ALL + k)
                at = piece(yy, 0)
                value = total[b, :, at, :, lanes(p)] + x_all[b, :, yy].astype(F32)
                total[b, :, at, :, lanes(p)] = value
                if k != 0:
                    total16[b, :, at, :, lanes(p)] = value.astype(BF16)
            copy(
                total16.at[b, :, piece(y_opp, 0), :, lanes(p)],
                far_in.at[b, 0, :, :, lanes(p)],
                b, p, Y_FAR, to_on,
            ).start()
            near(b, p, 1, 0, piece(y_off, 0), to_off)
            return
        x_out[b, :, :, lanes(p)] = y_sum(b, p, 1).astype(x_out.dtype)
        copy(
            x_out.at[b, :, :, lanes(p)], x_in.at[b, :, :, lanes(p)], b, p, X_SUM, to_x
        ).start()

    def spot(b, at, where):
        return acts.at[b, :, pl.ds(pl.multiple_of(at * span, span), span), where]

    def give(b, p, yy, which, kind, device):
        ref = spot(b, piece(yy, which), wide(p, core))
        copy(ref, ref, b, p, kind, device).start()

    def take(b, p, yy, which, kind, side):
        recv(spot(b, piece(yy, which), wide(p, side)), b, p, kind)

    def activate(b, p):
        value = y_sum(b, p, 0)
        if p != X_FIRST:
            recv(x_in.at[b, :, :, lanes(p)], b, p, X_SUM)
            value = value + x_in[b, :, :, lanes(p)].astype(F32)
        gate, up, grad_hidden = value[0], value[1], value[2]
        sig = jax.nn.sigmoid(gate)
        act = gate * sig
        at = pl.ds(pl.multiple_of(piece(y, 0) * span, span), span)
        where = wide(p, core)
        acts[b, 0, at, where] = (act * up).astype(BF16)
        acts[b, 1, at, where] = (grad_hidden * up * sig * (1.0 + gate * (1.0 - sig))).astype(BF16)
        acts[b, 2, at, where] = (grad_hidden * act).astype(BF16)
        give(b, p, y, 0, X_GIVE_ALL if p == X_FIRST else X_GIVE, to_x)
        give(b, p, y, 0, Y_GIVE, to_up)
        give(b, p, y, 0, Y_GIVE + 2, to_down)
        give(b, p, y, 0, CORE_GIVE, to_core)

    def give_second(b, p):
        take(b, p, y, 1, X_GIVE, core)
        give(b, p, y, 1, Y_GIVE + 1, to_up)
        give(b, p, y, 1, Y_GIVE + 3, to_down)
        give(b, p, y, 1, CORE_GIVE + 1, to_core)

    def swap(b, p, ks):
        for k in ks:
            take(b, p, chunks[k], 1, X_GIVE_ALL + k, core)
            give(b, p, chunks[k], 1, CORE_GIVE + 2 * k + 1, to_core)

    def swap_own(b, p):
        swap(b, p, (0,))

    def swap_near(b, p):
        swap(b, p, (1, 3))

    def swap_far(b, p):
        swap(b, p, (2,))

    def pass_on(b, p):
        take(b, p, y_down, 0, Y_GIVE, core)
        take(b, p, y_up, 0, Y_GIVE + 2, core)
        give(b, p, y_off, 0, Y_PASS, to_on)
        for k in (1, 3):
            give(b, p, chunks[k], 0, X_GIVE_ALL + k, to_x)
            give(b, p, chunks[k], 0, CORE_GIVE + 2 * k, to_core)

    def finish_on(b, p):
        take(b, p, y_opp, 0, Y_PASS, core)
        give(b, p, y_opp, 0, X_GIVE_ALL + 2, to_x)
        give(b, p, y_opp, 0, CORE_GIVE + 4, to_core)

    def pass_up(b, p):
        take(b, p, y_down, 0, Y_GIVE, core)
        give(b, p, y_down, 0, Y_PASS, to_up)
        give(b, p, y_down, 0, CORE_GIVE + 6, to_core)
        take(b, p, y_up, 0, Y_GIVE + 2, core)
        give(b, p, y_up, 0, CORE_GIVE + 2, to_core)

    def pass_down(b, p):
        take(b, p, y_up, 1, Y_GIVE + 3, core)
        give(b, p, y_up, 1, Y_PASS + 1, to_down)
        give(b, p, y_up, 1, CORE_GIVE + 3, to_core)
        take(b, p, y_down, 1, Y_GIVE + 1, core)
        give(b, p, y_down, 1, CORE_GIVE + 7, to_core)

    def finish(b, p):
        for which in range(2):
            take(b, p, y_opp, which, Y_PASS + which, core)
            give(b, p, y_opp, which, CORE_GIVE + 4 + which, to_core)

    def outputs(b, p):
        for p in range(len(PARTS)):
            for k, yy in enumerate((y, y_up, y_opp, y_down)):
                for which in range(2):
                    take(b, p, yy, which, CORE_GIVE + 2 * k + which, 1 - core)
        for i in range(2):
            if i == 0:
                value = nn(acts[b, 0], wd[...])
            else:
                value = nn(acts[b, 1], wg_flip[...]) + nn(acts[b, 2], wu_flip[...])
            if b == OWN:
                own_end[i] = value
            else:
                back_out[b, i] = value.astype(BF16)
                copy(
                    back_out.at[b, i], back_in.at[b, i], b, 0, BACK + i, to_row(-SHIFTS[b])
                ).start()

    def stores(b):
        at = pl.ds(b * toks, toks)
        hidden = turned_h.shape[1]
        return tuple(
            pltpu.make_async_copy(src, dst, out_sem.at[b, i])
            for i, (src, dst) in enumerate(
                (
                    (acts.at[b, pl.ds(1, 2)], acts_hbm.at[:, at]),
                    (turned_h.at[b], turned_hbm.at[b, pl.ds(0, hidden)]),
                    (turned_x.at[b], turned_hbm.at[b, pl.ds(hidden, turned_x.shape[1])]),
                    (rows.at[b, 1], cot_hbm.at[at]),
                )
            )
        )

    def turn(b, p):
        turned_x[b] = rows[b, 0].T

    def weights(b, p):
        at_once, after_turn, *rest = stores(b)
        at_once.start()
        for store in rest:
            store.start()
        turned_h[b] = acts[b, 0].T
        after_turn.start()

    tasks = dict(
        flip=flip,
        arrive=arrive,
        first=first,
        second=second,
        third=third,
        chip_sum=chip_sum,
        middle=middle,
        cross=cross,
        activate=activate,
        give_second=give_second,
        swap_own=swap_own,
        swap_near=swap_near,
        swap_far=swap_far,
        pass_on=pass_on,
        finish_on=finish_on,
        pass_up=pass_up,
        pass_down=pass_down,
        finish=finish,
        outputs=outputs,
        turn=turn,
        weights=weights,
    )
    for name, b, p in ORDER:
        tasks[name](b, p)

    for i in range(2):
        value = own_end[i]
        for b in range(STEPS):
            if b != OWN:
                recv(back_in.at[b, i], b, 0, BACK + i)
                value = value + back_in[b, i].astype(F32)
        ends[i] = value.astype(BF16)

    for b in range(STEPS):
        for p in range(len(PARTS)):
            if p == 0:
                for i in range(3):
                    sent(core_out.at[b, i], b, p, CORE_SUM + i)
            if p == X_FIRST:
                kinds = (Y_FAR, Y_NEAR, Y_NEAR + 2, Y_GIVE, Y_GIVE + 2, Y_PASS)
                kinds += tuple(range(X_SUM_ALL, KINDS)) + tuple(range(CORE_GIVE, BACK))
            else:
                kinds = tuple(range(Y_FAR, BACK))
            for kind in kinds:
                sent(spot(b, piece(y, 0), wide(p, core)), b, p, kind)
        if b != OWN:
            for i in range(2):
                sent(back_out.at[b, i], b, 0, BACK + i)
                sent(rows.at[b, i], b, 0, FETCH + i)

    for b in range(STEPS):
        for store in stores(b):
            store.wait()


def exchange(n_row, n_col, tokens, gate_weight, up_weight, down_weight, cotangent):
    toks, feats = tokens.shape
    hidden = gate_weight.shape[1]
    half = hidden // 2
    n_y = n_col // 4
    pieces = n_col // 2
    span = toks // pieces
    any_space = pl.BlockSpec(memory_space=pl.ANY)
    vmem = pl.BlockSpec(memory_space=pltpu.VMEM)
    return pl.pallas_call(
        functools.partial(exchange_kernel, n_row, n_y),
        out_shape=(
            jax.ShapeDtypeStruct((2, toks, feats), BF16),
            jax.ShapeDtypeStruct((2, STEPS * toks, hidden), BF16),
            jax.ShapeDtypeStruct((STEPS, hidden + feats, toks), BF16),
            jax.ShapeDtypeStruct((STEPS * toks, feats), BF16),
        ),
        in_specs=[any_space] * 5,
        out_specs=(vmem, any_space, any_space, any_space),
        scratch_shapes=[
            pltpu.VMEM(gate_weight.shape, BF16),
            pltpu.VMEM(up_weight.shape, BF16),
            pltpu.VMEM(down_weight.shape, BF16),
            pltpu.VMEM((hidden, feats), BF16),
            pltpu.VMEM((hidden, feats), BF16),
            pltpu.VMEM((feats, hidden), BF16),
            pltpu.VMEM((STEPS, 2, toks, feats), BF16),
            pltpu.VMEM((STEPS, 3, pieces, span, half), F32),
            pltpu.VMEM((STEPS, 3, pieces, span, half), F32),
            pltpu.VMEM((STEPS, 3, pieces, span, half), F32),
            pltpu.VMEM((STEPS, 3, pieces, span, half), BF16),
            pltpu.VMEM((STEPS, 2, 3, span, half), BF16),
            pltpu.VMEM((STEPS, 2, 2, 3, span, half), BF16),
            pltpu.VMEM((STEPS, 3, span, half), BF16),
            pltpu.VMEM((STEPS, 3, span, half), BF16),
            pltpu.VMEM((STEPS, 3, n_y, span, PARTS[X_FIRST][1]), BF16),
            pltpu.VMEM((STEPS, 3, toks, hidden), BF16),
            pltpu.VMEM((2, toks, feats), F32),
            pltpu.VMEM((STEPS, 2, toks, feats), BF16),
            pltpu.VMEM((STEPS, 2, toks, feats), BF16),
            pltpu.VMEM((STEPS, feats, toks), BF16),
            pltpu.VMEM((STEPS, hidden, toks), BF16),
            pltpu.SemaphoreType.DMA((STEPS, len(PARTS), KINDS)),
            pltpu.SemaphoreType.DMA((STEPS, len(PARTS), KINDS)),
            pltpu.SemaphoreType.DMA((8,)),
            pltpu.SemaphoreType.DMA((STEPS, 4)),
        ],
        compiler_params=pltpu.CompilerParams(
            collective_id=0, has_side_effects=True, vmem_limit_bytes=60 * 2**20
        ),
        name="exchange",
    )(tokens, gate_weight, up_weight, down_weight, cotangent)


def weight_kernel(
    ends_hbm,
    acts_hbm,
    turned_hbm,
    cot_hbm,
    mixed_hbm,
    tokens_hbm,
    gate_hbm,
    up_hbm,
    down_hbm,
    acts,
    turned,
    cot,
    ends,
    x,
    gate,
    up,
    down,
    in_sem,
    out_sem,
    end_sem,
):
    hidden = acts.shape[-1]
    toks = turned.shape[-1]
    copy = pltpu.make_async_copy
    tiles = [pl.ds(at, min(TILE, hidden - at)) for at in range(0, hidden, TILE)]
    tail = pl.ds(hidden, x.shape[0])
    load_x = copy(turned_hbm.at[:, tail], turned.at[:, tail], end_sem.at[0])
    load_cot = copy(cot_hbm, cot, end_sem.at[1])
    load_ends = copy(ends_hbm, ends, end_sem.at[2])
    load_acts = [copy(acts_hbm.at[k], acts.at[k], in_sem.at[0, k]) for k in range(2)]
    load_turned = [
        copy(turned_hbm.at[:, at], turned.at[:, at], in_sem.at[i, 2])
        for i, at in enumerate(tiles)
    ]
    for load in [load_x, *load_acts, load_cot, *load_turned, load_ends]:
        load.start()
    load_x.wait()
    for b in range(STEPS):
        x[:, b * toks : (b + 1) * toks] = turned[b, hidden:]
    stores = []

    def store(src, dst, sem):
        stores.append(copy(src, dst, sem))
        stores[-1].start()

    for k, (out, out_hbm) in enumerate(((gate, gate_hbm), (up, up_hbm))):
        load_acts[k].wait()
        out[...] = nn(x[...], acts[k]).astype(BF16)
        store(out, out_hbm, out_sem.at[0, k])
    load_cot.wait()
    for i, at in enumerate(tiles):
        load_turned[i].wait()
        h = jnp.concatenate([turned[b, at] for b in range(STEPS)], axis=1)
        down[at] = nn(h, cot[...]).astype(BF16)
        store(down.at[at], down_hbm.at[at], out_sem.at[i, 2])
    load_ends.wait()
    store(ends.at[0], mixed_hbm, end_sem.at[3])
    store(ends.at[1], tokens_hbm, end_sem.at[4])
    for out in stores:
        out.wait()


def weight_grads(ends, acts, turned, cot):
    _, toks, feats = ends.shape
    _, depth, hidden = acts.shape
    any_space = pl.BlockSpec(memory_space=pl.ANY)
    return pl.pallas_call(
        weight_kernel,
        out_shape=(
            jax.ShapeDtypeStruct((toks, feats), BF16),
            jax.ShapeDtypeStruct((toks, feats), BF16),
            jax.ShapeDtypeStruct((feats, hidden), BF16),
            jax.ShapeDtypeStruct((feats, hidden), BF16),
            jax.ShapeDtypeStruct((hidden, feats), BF16),
        ),
        in_specs=[any_space] * 4,
        out_specs=(any_space,) * 5,
        scratch_shapes=[
            pltpu.VMEM(acts.shape, BF16),
            pltpu.VMEM(turned.shape, BF16),
            pltpu.VMEM(cot.shape, BF16),
            pltpu.VMEM(ends.shape, BF16),
            pltpu.VMEM((feats, depth), BF16),
            pltpu.VMEM((feats, hidden), BF16),
            pltpu.VMEM((feats, hidden), BF16),
            pltpu.VMEM((hidden, feats), BF16),
            pltpu.SemaphoreType.DMA((pl.cdiv(hidden, TILE), 3)),
            pltpu.SemaphoreType.DMA((pl.cdiv(hidden, TILE), 3)),
            pltpu.SemaphoreType.DMA((5,)),
        ],
        compiler_params=pltpu.CompilerParams(vmem_limit_bytes=60 * 2**20),
        name="weight_grads",
    )(ends, acts, turned, cot)


def solution(mesh):
    n_row, n_col = mesh.shape["row"], mesh.shape["col"]
    placed = (P("row", "col"), P("col", "row"), P("col", "row"), P("row", "col"), P("row", "col"))

    def body(tokens, gate_weight, up_weight, down_weight, cotangent):
        return weight_grads(
            *exchange(n_row, n_col, tokens, gate_weight, up_weight, down_weight, cotangent)
        )

    return jax.shard_map(
        body,
        mesh=mesh,
        in_specs=placed,
        out_specs=(
            P("row", "col"),
            P("row", "col"),
            P("col", "row"),
            P("col", "row"),
            P("row", "col"),
        ),
        check_vma=False,
    )
```
